256 devices in a mesh: sec: 16 (over y, x), term: 16 (over z, core).
Axes of the slice: x: 4, y: 4, z: 8, core: 2. Of those that a mesh axis runs over, the one named last changes fastest.
Arguments:
- initial: float32 [8192, 512], P(('sec', 'term')), may hold values from -6 to 6
- onsite: float32 [8192, 512], P(('sec', 'term')), may hold values from 0.5 to 4
- left_env: float32 [16, 32, 512, 512], P('sec', 'term'), as said below
- right_env: float32 [16, 32, 512, 512], P('sec', 'term'), as said below
- sector_dims: int32 [16, 2], P('sec'), may hold values from 128 to 512, as said below
Outputs:
- block_vector: float32 [8192, 512], P(('sec', 'term'))
- energies: float32 [16], P('sec')
The draws below stay inside these ranges and needn't reach their ends.
Inputs may be any that keep to these rules, and one draw needn't show every extreme that they name: `sector_dims`: at least one entry equals 512. `left_env`: each [section, term] matrix is symmetric. `right_env`: each [section, term] matrix is symmetric.
All inputs are finite; a program needn't handle non-finite values.
Results may differ from the reference program's by a relative error of at most 0.0003.
Values sent between devices are 32-bit elements; how exact they have to be, the bound alone decides.
A program may use at most 64 MiB of HBM per device.

```python
import math
import jax
import jax.numpy as jnp
from jax import lax

PAD = 512
ITERS = 4
TERMS = 32
SECTIONS = 16


def shape_env(raw, line_key):
    symmetric = (raw + jnp.swapaxes(raw, -1, -2)) * 0.5 ** 0.5
    spread = jnp.exp(jax.random.uniform(line_key, (SECTIONS, TERMS, PAD), jnp.float32, -1.15, 1.15)) / 1.47
    scaled = symmetric * spread[:, :, :, None] * spread[:, :, None, :]
    return scaled * PAD ** (-0.5) * TERMS ** (-0.25)


def draw_left_env(key, part):
    key = jax.random.fold_in(key, 1)
    raw_key = jax.random.fold_in(key, 11)
    line_key = jax.random.fold_in(key, 12)
    raw = jax.random.normal(raw_key, (SECTIONS, TERMS, PAD, PAD), jnp.float32)
    return shape_env(raw, line_key).astype(jnp.float32)


def draw_right_env(key, part):
    key = jax.random.fold_in(key, 2)
    raw_key = jax.random.fold_in(key, 21)
    line_key = jax.random.fold_in(key, 22)
    raw = jax.random.normal(raw_key, (SECTIONS, TERMS, PAD, PAD), jnp.float32)
    return shape_env(raw, line_key).astype(jnp.float32)


def draw_sector_dims(key, part):
    key = jax.random.fold_in(key, 3)
    values = jax.random.randint(jax.random.fold_in(key, 31), (SECTIONS * 2,), PAD // 4, PAD + 1)
    chosen = jax.random.randint(jax.random.fold_in(key, 32), (), 0, SECTIONS * 2)
    filled = jnp.where(jnp.arange(SECTIONS * 2) == chosen, PAD, values)
    return filled.reshape(SECTIONS, 2).astype(jnp.int32)


def block_levels(key, shape, pieces, low, high):
    factor_of, own = 1.0, jax.random.fold_in(key, 6)
    for position, parts in pieces:
        steps = jnp.exp(jax.random.uniform(jax.random.fold_in(own, position), (parts,), jnp.float32, low / len(pieces), high / len(pieces)))
        factor_of = factor_of * jnp.repeat(steps, shape[position] // parts).reshape([-1 if axis == position else 1 for axis in range(len(shape))])
    return factor_of


def gaussian(stream_key, extent, width, most, pieces=(), kind=jnp.bfloat16):
    array = jax.random.normal(stream_key, extent, jnp.float32) * width
    if len(pieces) > 0:
        array = block_levels(stream_key, extent, pieces, -0.22, 0.18) * array
    return jnp.clip(array, min=-most, max=most).astype(kind)


def setup_inputs(seed: int = 0) -> dict:
    key_of = jax.random.split(jax.random.key(seed), 6)
    initial = gaussian(key_of[0], (SECTIONS * PAD, PAD), 1.0, 6.0, ((0, 256),), jnp.float32)
    onsite = jnp.clip(jnp.exp(math.log(4.0) - 2.0794415 * jax.random.uniform(key_of[1], (SECTIONS * PAD, PAD), jnp.float32) ** block_levels(key_of[1], (SECTIONS * PAD, PAD), ((0, 256),), -0.2, 0.2)), 0.5, 4.0)
    left_env = draw_left_env(jax.random.fold_in(key_of[5], 71), 0)
    right_env = draw_right_env(jax.random.fold_in(key_of[5], 71), 0)
    sector_dims = draw_sector_dims(jax.random.fold_in(key_of[5], 71), 0)
    return dict(initial=initial, onsite=onsite, left_env=left_env, right_env=right_env, sector_dims=sector_dims)


def section_solve(index, initial, onsite, left_env, right_env, sector_dims):
    left_terms = left_env[index]
    following = jnp.minimum(index + 1, SECTIONS - 1).astype(jnp.int32)
    present = (index + 1 < SECTIONS).astype(jnp.float32)
    right_terms = right_env[following] * present
    sector_pair = sector_dims[index]
    line_index = jnp.arange(PAD, dtype=jnp.int32)
    live_mask = ((line_index < sector_pair[0])[:, None] & (line_index < sector_pair[1])[None, :]).astype(jnp.float32)
    first_row = (index * PAD).astype(jnp.int32)
    start_block = lax.dynamic_slice_in_dim(initial, first_row, PAD, 0)
    site_block = lax.dynamic_slice_in_dim(onsite, first_row, PAD, 0)

    def operate(vector_in):

        def add_term(term_index, accum):
            carried = jnp.dot(vector_in, right_terms[term_index], precision=lax.Precision.HIGHEST)
            return accum + jnp.dot(left_terms[term_index], carried, precision=lax.Precision.HIGHEST)
        summed = lax.fori_loop(0, TERMS, add_term, jnp.zeros((PAD, PAD), jnp.float32))
        return live_mask * (summed + site_block * vector_in)
    masked = live_mask * start_block
    estimate = masked / jnp.sqrt(jnp.sum(masked * masked))
    image = operate(estimate)
    ritz_value = jnp.sum(estimate * image)
    for iteration in range(ITERS):
        residual = image - ritz_value * estimate
        res_square = jnp.sum(residual * residual)
        direction = residual / jnp.sqrt(res_square)
        turned = operate(direction)
        bend_value = jnp.sum(direction * turned)
        half_gap = 0.5 * (bend_value - ritz_value)
        radius = jnp.sqrt(half_gap * half_gap + res_square)
        step_size = -jnp.sqrt(res_square) / (half_gap + radius)
        scale_back = jnp.sqrt(1.0 + step_size * step_size)
        estimate = (estimate + step_size * direction) / scale_back
        image = (image + step_size * turned) / scale_back
        ritz_value = ritz_value + half_gap - radius
    return (estimate * (0.5 * PAD), ritz_value)

def reference(initial, onsite, left_env, right_env, sector_dims):

    def solve_one(index):
        return section_solve(index, initial, onsite, left_env, right_env, sector_dims)
    blocks, energies = lax.map(solve_one, jnp.arange(SECTIONS, dtype=jnp.int32))
    return (blocks.reshape(SECTIONS * PAD, PAD), energies)
```

```python
import functools

import jax
import jax.numpy as jnp
from jax import lax
from jax.experimental import pallas as pl
from jax.experimental.pallas import tpu as pltpu
from jax.sharding import PartitionSpec as P

ITERS = 4
PAD = 512
HALF = 256
TILE = 128
RING = 8
SECTIONS = 16
ROWS = PAD // RING
MESH = pl.DeviceIdType.MESH
F32, BF16 = jnp.float32, jnp.bfloat16


def dot(a, b):
    return jnp.dot(a, b, preferred_element_type=F32)


def split(x):
    high = x.astype(BF16)
    return high, (x - high.astype(F32)).astype(BF16)


def kernel(
    init_ref, site_ref, left_ref, right_ref, dims_ref, out_ref, energy_ref,
    lstage, lhi, llo, rdiag, roff, rhi, rlo, chi, clo,
    start, site, turned, estimate, image, resid, vhi, vlo, part, rsbuf, scal,
    lsem, lsend, lrecv, insend, inrecv, rsend, drecv, brecv, bfwd,
    rs_send, rs_recv, ag_send, ag_recv, cross_send, cross_recv, sc_send, sc_recv,
):
    s, t = lax.axis_index("sec"), lax.axis_index("term")
    z, c = t // 2, t % 2
    sign = 2 * c - 1

    def chip(k):
        return lax.rem(z + sign * k + 2 * RING, RING)

    def on_ring(k):
        return (s, chip(k) * 2 + c)

    other = (s, z * 2 + 1 - c)
    before = lax.rem(s + SECTIONS - 1, SECTIONS)
    after = lax.rem(s + 1, SECTIONS)

    def rows_of(chip_index):
        return pl.ds(pl.multiple_of(chip_index * ROWS, ROWS), ROWS)

    def remote(src, dst, send, recv, to):
        return pltpu.make_async_remote_copy(
            src_ref=src, dst_ref=dst, send_sem=send, recv_sem=recv,
            device_id=to, device_id_type=MESH,
        )

    local_left = [
        pltpu.make_async_copy(left_ref.at[0, j], lstage.at[2 * j], lsem.at[j])
        for j in range(2)
    ]
    for cp in local_left:
        cp.start()

    barrier = pltpu.get_barrier_semaphore()
    for k in range(1, 2 * RING):
        pl.semaphore_signal(
            barrier, inc=1, device_id=(s, lax.rem(t + k, 2 * RING)), device_id_type=MESH)
    for k in range(2):
        pl.semaphore_signal(
            barrier, inc=1, device_id=(after, z * 2 + k), device_id_type=MESH)
    pl.semaphore_wait(barrier, 2 * RING + 1)

    own_cols = pl.ds(pl.multiple_of(c * HALF, HALF), HALF)
    other_cols = pl.ds(pl.multiple_of((1 - c) * HALF, HALF), HALF)
    my_rows = pl.ds(pl.multiple_of(c * (ROWS // 2), ROWS // 2), ROWS // 2)
    peer_rows = pl.ds(pl.multiple_of((1 - c) * (ROWS // 2), ROWS // 2), ROWS // 2)
    inputs = [
        remote(ref.at[:, other_cols], buf.at[my_rows], insend.at[k], inrecv.at[k], other)
        for k, (ref, buf) in enumerate(((init_ref, start), (site_ref, site)))
    ]
    for cp in inputs:
        cp.start()

    def diag_copies(j, own):
        base = (c if own else 1 - c) * HALF
        slot = 2 * j + (0 if own else 1)
        to = (before, z * 2 + (c if own else 1 - c))
        out = []
        for m, (height, shift) in enumerate(((TILE, 0), (TILE, TILE))):
            r0 = pl.multiple_of(base + m * TILE, TILE)
            c0 = pl.multiple_of(base + shift, TILE)
            out.append(remote(
                right_ref.at[0, j, pl.ds(r0, height), pl.ds(c0, HALF - shift)],
                rdiag.at[slot, pl.ds(m * TILE, height), pl.ds(shift, HALF - shift)],
                rsend.at[j, 2 * (0 if own else 1) + m], drecv.at[slot, m], to))
        return out

    def off_copy(j):
        return remote(
            right_ref.at[0, j, pl.ds(0, HALF), pl.ds(HALF, HALF)], roff.at[2 * j],
            rsend.at[j, 4], brecv.at[2 * j], (before, t))

    def off_forward(j):
        return remote(
            roff.at[2 * j], roff.at[2 * j + 1], bfwd.at[j], brecv.at[2 * j + 1], other)

    shifts = [[off_copy(j)] + diag_copies(j, True) + diag_copies(j, False) for j in range(2)]
    for group in shifts:
        for cp in group:
            cp.start()
    left_cross = [
        remote(left_ref.at[0, j], lstage.at[2 * j + 1], lsend.at[j], lrecv.at[j], other)
        for j in range(2)
    ]
    for cp in left_cross:
        cp.start()

    row_index = lax.broadcasted_iota(jnp.int32, (ROWS, HALF), 0) + z * ROWS
    col_index = lax.broadcasted_iota(jnp.int32, (ROWS, HALF), 1) + c * HALF
    live = jnp.where(
        (row_index < dims_ref[0, 0]) & (col_index < dims_ref[0, 1]), 1.0, 0.0).astype(F32)

    own_rows = rows_of(z)

    def gather(n):
        def ring_copy(k, src_chip, index):
            part_ref = turned.at[n, 0, rows_of(src_chip)]
            return remote(part_ref, part_ref, ag_send.at[n, index], ag_recv.at[n, index],
                          on_ring(k))

        def cross_copy(k):
            return remote(turned.at[n, 0, rows_of(chip(k))], turned.at[n, 1, rows_of(chip(k))],
                          cross_send.at[n, k % RING], cross_recv.at[n, k % RING], other)

        def cross_wait(k):
            rows = rows_of(chip(-k))
            remote(turned.at[n, 0, rows], turned.at[n, 1, rows],
                   cross_send.at[n, k % RING], cross_recv.at[n, k % RING], other).wait_recv()

        plus2, minus2 = ring_copy(2, z, 0), ring_copy(-2, z, 1)
        plus1, minus1 = ring_copy(1, z, 2), ring_copy(-1, z, 3)
        for cp in (plus2, minus2, plus1, minus1):
            cp.start()
        sends = [plus2, minus2, plus1, minus1]

        def received(index, k):
            part_ref = turned.at[n, 0, rows_of(chip(k))]
            remote(part_ref, part_ref, ag_send.at[n, index], ag_recv.at[n, index],
                   on_ring(k)).wait_recv()

        crosses = [cross_copy(0)]
        crosses[-1].start()

        def cross(k):
            crosses.append(cross_copy(k))
            crosses[-1].start()

        received(0, -2)
        for cp in (ring_copy(1, chip(-2), 4), ring_copy(2, chip(-2), 5)):
            cp.start()
            sends.append(cp)
        received(1, 2)
        cp = ring_copy(-1, chip(2), 6)
        cp.start()
        sends.append(cp)
        cross(-2)
        cross(2)
        received(2, -1)
        cross(-1)
        received(3, 1)
        cross(1)
        received(4, -3)
        cross(-3)
        received(6, 3)
        cross(3)
        received(5, -4)
        cross(-4)
        for k in (0, -2, 2, -1, 1, -3, 3, -4):
            cross_wait(k)
        for cp in sends + crosses:
            cp.wait_send()

    def block(j):
        return part.at[pl.ds(j * ROWS, ROWS)]

    def reduce(n):
        def send(src, slot, k):
            cp = remote(src, rsbuf.at[n, slot], rs_send.at[n, slot], rs_recv.at[n, slot],
                        on_ring(k))
            cp.start()
            return cp

        def wait(slot):
            remote(block(0), rsbuf.at[n, slot], rs_send.at[n, slot], rs_recv.at[n, slot],
                   on_ring(1)).wait_recv()

        sends = [
            send(block(4), 1, 2), send(block(3), 0, 1), send(block(5), 2, -1),
            send(block(1), 3, 1), send(block(7), 4, -1),
        ]
        wait(0)
        wait(1)
        block(2)[...] = block(2)[...] + rsbuf[n, 0] + rsbuf[n, 1]
        sends.append(send(block(2), 5, 2))
        wait(2)
        block(6)[...] = block(6)[...] + rsbuf[n, 2]
        sends.append(send(block(6), 6, -2))
        wait(3)
        wait(4)
        total = block(0)[...] + rsbuf[n, 3] + rsbuf[n, 4]
        wait(5)
        wait(6)
        total = total + rsbuf[n, 5] + rsbuf[n, 6]
        for cp in sends:
            cp.wait_send()
        return total

    def carry(q):
        acc = (dot(vhi[0], rhi[q, 0]) + dot(vhi[1], rhi[q, 1])
               + dot(vlo[0], rhi[q, 0]) + dot(vlo[1], rhi[q, 1])
               + dot(vhi[0], rlo[q, 0]) + dot(vhi[1], rlo[q, 1]))
        chi[q], clo[q] = split(acc)

    def bring_back(q):
        return dot(lhi[q], chi[q]) + dot(llo[q], chi[q]) + dot(lhi[q], clo[q])

    def operate():
        for q in range(4):
            carry(q)
        part[...] = (bring_back(0) + bring_back(1)) + (bring_back(2) + bring_back(3))

    CHUNK = 64

    def over_chunks(body, sums):
        totals = [[], []]
        for half in range(2):
            def step(i, acc, half=half):
                rows = pl.ds(pl.multiple_of(i * CHUNK, CHUNK), CHUNK)
                values = body(half, rows)
                return tuple(
                    a + jnp.sum(v.reshape(CHUNK // 8, 8, HALF), axis=0)
                    for a, v in zip(acc, values))
            zero = tuple(jnp.zeros((8, HALF), F32) for _ in range(sums))
            acc = lax.fori_loop(0, PAD // CHUNK, step, zero, unroll=2)
            totals[half] = [jnp.sum(a, axis=(0, 1), keepdims=True) for a in acc]
        return [a + b for a, b in zip(*totals)]

    for cp in inputs:
        cp.wait_send()
    inputs_in = [
        remote(buf.at[peer_rows], buf.at[peer_rows], insend.at[k], inrecv.at[k], other)
        for k, buf in enumerate((start, site))
    ]
    for cp in inputs_in:
        cp.wait_recv()
    start[my_rows] = init_ref[:, own_cols]
    turned[0, 0, own_rows] = live * start[...]
    site[my_rows] = site_ref[:, own_cols]
    gather(0)

    def first_split(half, rows):
        u = turned[0, half, rows]
        vhi[half, rows], vlo[half, rows] = split(u)
        return (u * u,)

    (norm_square,) = over_chunks(first_split, 1)

    for j in range(2):
        local_left[j].wait()
        left_cross[j].wait()
    for q in range(4):
        for k in range(RING):
            hi, lo = split(lstage[q, rows_of(chip(k))])
            lhi[q, pl.ds(k * ROWS, ROWS)] = hi
            llo[q, pl.ds(k * ROWS, ROWS)] = lo

    present = jnp.where(s + 1 < SECTIONS, 1.0, 0.0).astype(F32)

    def prepare(q):
        for m, shift in ((0, 0), (1, TILE)):
            piece = rdiag.at[q, pl.ds(m * TILE, TILE), pl.ds(shift, HALF - shift)]
            remote(piece, piece, rsend.at[0, 0], drecv.at[q, m], other).wait_recv()
        top = rdiag[q, pl.ds(0, TILE), :] * present
        low = rdiag[q, pl.ds(TILE, TILE), pl.ds(TILE, TILE)] * present
        hi, lo = split(top)
        rhi[q, 0, pl.ds(0, TILE), :] = hi
        rlo[q, 0, pl.ds(0, TILE), :] = lo
        hi, lo = split(top[:, TILE:].T)
        rhi[q, 0, pl.ds(TILE, TILE), pl.ds(0, TILE)] = hi
        rlo[q, 0, pl.ds(TILE, TILE), pl.ds(0, TILE)] = lo
        hi, lo = split(low)
        rhi[q, 0, pl.ds(TILE, TILE), pl.ds(TILE, TILE)] = hi
        rlo[q, 0, pl.ds(TILE, TILE), pl.ds(TILE, TILE)] = lo

        @pl.when(c == 0)
        def _():
            rhi[q, 1], rlo[q, 1] = split((roff[q] * present).T)

        @pl.when(c == 1)
        def _():
            rhi[q, 1], rlo[q, 1] = split(roff[q] * present)

    for j in range(2):
        off_copy(j).wait_recv()
        forward = off_forward(j)
        forward.start()
        prepare(2 * j)
        carry(2 * j)
        forward.wait()
        prepare(2 * j + 1)
        carry(2 * j + 1)
        fresh = bring_back(2 * j) + bring_back(2 * j + 1)
        if j == 0:
            part[...] = fresh
        else:
            part[...] = part[...] + fresh
    for group in shifts:
        for cp in group:
            cp.wait_send()

    def image_rows(n, vector):
        own = reduce(n)
        turned[n + 1, 0, own_rows] = live * (own + site[...] * vector)
        gather(n + 1)

    image_rows(0, turned[0, 0, own_rows])
    inverse = 1.0 / jnp.sqrt(norm_square)

    def first_ritz(half, rows):
        est = turned[0, half, rows] * inverse
        img = turned[1, half, rows] * inverse
        estimate[half, rows] = est
        image[half, rows] = img
        return (est * img,)

    (ritz,) = over_chunks(first_ritz, 1)

    def first_residual(half, rows):
        res = image[half, rows] - ritz * estimate[half, rows]
        resid[half, rows] = res
        vhi[half, rows], vlo[half, rows] = split(res)
        return (res * res,)

    (res_square,) = over_chunks(first_residual, 1)

    def coefficients(ritz, res_square, bend):
        half_gap = 0.5 * (bend - ritz)
        radius = jnp.sqrt(half_gap * half_gap + res_square)
        step = -jnp.sqrt(res_square) / (half_gap + radius)
        back = 1.0 / jnp.sqrt(1.0 + step * step)
        return step, back, ritz + half_gap - radius

    def iterate(n, carried):
        ritz, res_square = carried
        operate()
        image_rows(n, resid[0, own_rows])
        inverse = 1.0 / jnp.sqrt(res_square)

        def bends(half, rows):
            return ((resid[half, rows] * inverse) * (turned[n + 1, half, rows] * inverse),)

        (bend,) = over_chunks(bends, 1)
        step, back, new_ritz = coefficients(ritz, res_square, bend)
        scaled = step * inverse

        def update(half, rows):
            est = (estimate[half, rows] + scaled * resid[half, rows]) * back
            img = (image[half, rows] + scaled * turned[n + 1, half, rows]) * back
            estimate[half, rows] = est
            image[half, rows] = img
            res = img - new_ritz * est
            resid[half, rows] = res
            vhi[half, rows], vlo[half, rows] = split(res)
            return (res * res,)

        (new_square,) = over_chunks(update, 1)
        return new_ritz, new_square

    ritz, res_square = lax.fori_loop(1, ITERS, iterate, (ritz, res_square))

    operate()
    inverse = 1.0 / jnp.sqrt(res_square)
    acc = site[...] * (resid[0, own_rows] * inverse) * (resid[0, own_rows] * inverse)
    for k in range(RING):
        acc = acc + (block(k)[...] * inverse) * (resid[0, rows_of(chip(k))] * inverse)
    mine = jnp.sum(acc, axis=(0, 1), keepdims=True)
    scal[t] = jnp.broadcast_to(mine, (8, 128))
    bends = []
    for k in range(1, 2 * RING):
        cp = remote(scal.at[t], scal.at[t], sc_send.at[k], sc_recv.at[k],
                    (s, lax.rem(t + k, 2 * RING)))
        cp.start()
        bends.append(cp)
    for k in range(1, 2 * RING):
        slot = scal.at[lax.rem(t + 2 * RING - k, 2 * RING)]
        remote(slot, slot, sc_send.at[k], sc_recv.at[k], other).wait_recv()
    bend = jnp.sum(scal[...], axis=0)[0:1, 0:1]
    step, back, ritz = coefficients(ritz, res_square, bend)
    scaled = step * inverse
    out_rows = pl.ds(pl.multiple_of(t * (ROWS // 2), ROWS // 2), ROWS // 2)
    for half, cols in ((0, own_cols), (1, other_cols)):
        est = (estimate[half, out_rows] + scaled * resid[half, out_rows]) * back
        out_ref[:, cols] = est * (0.5 * PAD)
    energy_ref[0] = ritz[0, 0]
    for cp in bends:
        cp.wait_send()


def per_device(initial, onsite, left_env, right_env, sector_dims):
    vmem = pl.BlockSpec(memory_space=pltpu.VMEM)
    smem = pl.BlockSpec(memory_space=pltpu.SMEM)
    anywhere = pl.BlockSpec(memory_space=pl.ANY)
    dma = pltpu.SemaphoreType.DMA
    full = (2, PAD, HALF)
    return pl.pallas_call(
        kernel,
        out_shape=(
            jax.ShapeDtypeStruct((ROWS // 2, PAD), F32),
            jax.ShapeDtypeStruct((1,), F32),
        ),
        in_specs=[vmem, vmem, anywhere, anywhere, smem],
        out_specs=(vmem, smem),
        scratch_shapes=[
            pltpu.VMEM((4, PAD, PAD), F32),
            pltpu.VMEM((4, PAD, PAD), BF16),
            pltpu.VMEM((4, PAD, PAD), BF16),
            pltpu.VMEM((4, HALF, HALF), F32),
            pltpu.VMEM((4, HALF, HALF), F32),
            pltpu.VMEM((4, 2, HALF, HALF), BF16),
            pltpu.VMEM((4, 2, HALF, HALF), BF16),
            pltpu.VMEM((4, PAD, HALF), BF16),
            pltpu.VMEM((4, PAD, HALF), BF16),
            pltpu.VMEM((ROWS, HALF), F32),
            pltpu.VMEM((ROWS, HALF), F32),
            pltpu.VMEM((ITERS + 1,) + full, F32),
            pltpu.VMEM(full, F32),
            pltpu.VMEM(full, F32),
            pltpu.VMEM(full, F32),
            pltpu.VMEM(full, BF16),
            pltpu.VMEM(full, BF16),
            pltpu.VMEM((PAD, HALF), F32),
            pltpu.VMEM((ITERS, 7, ROWS, HALF), F32),
            pltpu.VMEM((2 * RING, 8, 128), F32),
            dma((2,)), dma((2,)), dma((2,)), dma((2,)), dma((2,)),
            dma((2, 5)), dma((4, 2)), dma((4,)), dma((2,)),
            dma((ITERS, 7)), dma((ITERS, 7)),
            dma((ITERS + 1, 7)), dma((ITERS + 1, 7)),
            dma((ITERS + 1, RING)), dma((ITERS + 1, RING)),
            dma((2 * RING,)), dma((2 * RING,)),
        ],
        compiler_params=pltpu.CompilerParams(
            collective_id=0, has_side_effects=True, vmem_limit_bytes=56 * 2**20),
        cost_estimate=pl.CostEstimate(
            flops=5 * 3 * 2 * 4 * 2 * PAD * PAD * HALF, bytes_accessed=2**23, transcendentals=0),
    )(initial, onsite, left_env, right_env, sector_dims)


def solution(mesh):
    return jax.shard_map(
        per_device,
        mesh=mesh,
        in_specs=(
            P(("sec", "term"), None),
            P(("sec", "term"), None),
            P("sec", "term", None, None),
            P("sec", "term", None, None),
            P("sec", None),
        ),
        out_specs=(P(("sec", "term"), None), P("sec")),
        check_vma=False,
    )
```

```python
import functools

import jax
import jax.numpy as jnp
from jax import lax
from jax.experimental import pallas as pl
from jax.experimental.pallas import tpu as pltpu
from jax.sharding import PartitionSpec as P

ITERS = 4
PAD = 512
HALF = 256
TILE = 128
RING = 8
SECTIONS = 16
ROWS = PAD // RING
MESH = pl.DeviceIdType.MESH
F32, BF16 = jnp.float32, jnp.bfloat16


def dot(a, b):
    return jnp.dot(a, b, preferred_element_type=F32)


def split(x):
    high = x.astype(BF16)
    return high, (x - high.astype(F32)).astype(BF16)


def kernel(
    init_ref, site_ref, left_ref, right_ref, dims_ref, out_ref, energy_ref,
    lstage, lhi, llo, rdiag, roff, rhi, rlo, chi, clo,
    start, site, turned, estimate, image, resid, vhi, vlo, part, rsbuf, scal,
    lsem, lsend, lrecv, insend, inrecv, rsend, drecv, brecv, bfwd,
    rs_send, rs_recv, ag_send, ag_recv, cross_send, cross_recv, sc_send, sc_recv,
):
    s, t = lax.axis_index("sec"), lax.axis_index("term")
    z, c = t // 2, t % 2
    sign = 2 * c - 1

    def chip(k):
        return lax.rem(z + sign * k + 2 * RING, RING)

    def on_ring(k):
        return (s, chip(k) * 2 + c)

    other = (s, z * 2 + 1 - c)
    before = lax.rem(s + SECTIONS - 1, SECTIONS)
    after = lax.rem(s + 1, SECTIONS)

    def rows_of(chip_index):
        return pl.ds(pl.multiple_of(chip_index * ROWS, ROWS), ROWS)

    def remote(src, dst, send, recv, to):
        return pltpu.make_async_remote_copy(
            src_ref=src, dst_ref=dst, send_sem=send, recv_sem=recv,
            device_id=to, device_id_type=MESH,
        )

    local_left = [
        pltpu.make_async_copy(left_ref.at[0, j], lstage.at[2 * j], lsem.at[j])
        for j in range(2)
    ]
    for cp in local_left:
        cp.start()

    barrier = pltpu.get_barrier_semaphore()
    for k in range(1, 2 * RING):
        pl.semaphore_signal(
            barrier, inc=1, device_id=(s, lax.rem(t + k, 2 * RING)), device_id_type=MESH)
    for k in range(2):
        pl.semaphore_signal(
            barrier, inc=1, device_id=(after, z * 2 + k), device_id_type=MESH)
    pl.semaphore_wait(barrier, 2 * RING + 1)

    own_cols = pl.ds(pl.multiple_of(c * HALF, HALF), HALF)
    other_cols = pl.ds(pl.multiple_of((1 - c) * HALF, HALF), HALF)
    my_rows = pl.ds(pl.multiple_of(c * (ROWS // 2), ROWS // 2), ROWS // 2)
    peer_rows = pl.ds(pl.multiple_of((1 - c) * (ROWS // 2), ROWS // 2), ROWS // 2)
    inputs = [
        remote(ref.at[:, other_cols], buf.at[my_rows], insend.at[k], inrecv.at[k], other)
        for k, (ref, buf) in enumerate(((init_ref, start), (site_ref, site)))
    ]
    for cp in inputs:
        cp.start()

    def diag_copy(j, own, piece):
        column = c if own else 1 - c
        slot = 2 * j + (0 if own else 1)
        r0 = pl.multiple_of(column * HALF + piece * TILE, TILE)
        width = HALF - piece * TILE
        return remote(
            right_ref.at[0, j, pl.ds(r0, TILE), pl.ds(r0, width)],
            rdiag.at[slot, pl.ds(piece * TILE, TILE), pl.ds(piece * TILE, width)],
            rsend.at[j, (0 if own else 2) + piece], drecv.at[slot, piece],
            (before, z * 2 + column))

    off_parts = ((0, 0, HALF), (TILE, 0, TILE), (TILE, TILE, TILE))

    def off_piece(slot, piece):
        r0, c0, width = off_parts[piece]
        return roff.at[slot, pl.ds(r0, TILE), pl.ds(c0, width)]

    def off_copy(j, piece):
        r0, c0, width = off_parts[piece]
        return remote(
            right_ref.at[0, j, pl.ds(r0, TILE), pl.ds(HALF + c0, width)],
            off_piece(2 * j, piece), rsend.at[j, 4 + piece], brecv.at[2 * j, piece],
            (before, t))

    def off_forward(j, piece):
        return remote(off_piece(2 * j, piece), off_piece(2 * j + 1, piece),
                      bfwd.at[j, piece], brecv.at[2 * j + 1, piece], other)

    shifts = []
    for j in range(2):
        shifts += [off_copy(j, 0), off_copy(j, 1), diag_copy(j, True, 0), diag_copy(j, False, 0)]
    for j in range(2):
        shifts += [off_copy(j, 2), diag_copy(j, True, 1), diag_copy(j, False, 1)]
    for cp in shifts:
        cp.start()
    left_cross = [
        remote(left_ref.at[0, j], lstage.at[2 * j + 1], lsend.at[j], lrecv.at[j], other)
        for j in range(2)
    ]
    for cp in left_cross:
        cp.start()

    row_index = lax.broadcasted_iota(jnp.int32, (ROWS, HALF), 0) + z * ROWS
    col_index = lax.broadcasted_iota(jnp.int32, (ROWS, HALF), 1) + c * HALF
    live = jnp.where(
        (row_index < dims_ref[0, 0]) & (col_index < dims_ref[0, 1]), 1.0, 0.0).astype(F32)

    own_rows = rows_of(z)

    def gather_start(n, u):
        def ring_copy(k, src_chip, index):
            piece = turned.at[n, 0, u, rows_of(src_chip)]
            return remote(piece, piece, ag_send.at[n, u], ag_recv.at[n, u, index], on_ring(k))

        def cross(k):
            rows = rows_of(chip(k))
            remote(turned.at[n, 0, u, rows], turned.at[n, 1, u, rows],
                   cross_send.at[n, u], cross_recv.at[n, u], other).start()

        def received(index, k):
            piece = turned.at[n, 0, u, rows_of(chip(k))]
            remote(piece, piece, ag_send.at[n, u], ag_recv.at[n, u, index],
                   on_ring(k)).wait_recv()

        ring_copy(2, z, 0).start()
        ring_copy(-2, z, 1).start()
        ring_copy(1, z, 2).start()
        ring_copy(-1, z, 3).start()
        cross(0)

        def forward():
            received(0, -2)
            ring_copy(2, chip(-2), 5).start()
            ring_copy(1, chip(-2), 4).start()
            received(1, 2)
            ring_copy(-1, chip(2), 6).start()
            cross(-2)
            cross(2)
            received(2, -1)
            cross(-1)
            received(3, 1)
            cross(1)

        def finish():
            received(4, -3)
            cross(-3)
            received(6, 3)
            cross(3)
            received(5, -4)
            cross(-4)
            other_half = turned.at[n, 1, u]
            remote(other_half, other_half, cross_send.at[n, u], cross_recv.at[n, u],
                   other).wait_recv()

        return forward, finish

    def gather_sent(n, u):
        seven = rsbuf.at[0, 0]
        remote(seven, seven, ag_send.at[n, u], ag_recv.at[n, u, 0], other).wait_send()
        half = turned.at[n, 0, u]
        remote(half, half, cross_send.at[n, u], cross_recv.at[n, u], other).wait_send()

    def block(u, j):
        return part.at[u, pl.ds((j + 6) % RING * ROWS, ROWS)]

    def reduce_send(n, u, src, slot, k):
        remote(src, rsbuf.at[n, u, slot], rs_send.at[n, u], rs_recv.at[n, u, slot],
               on_ring(k)).start()

    def reduce_wait(n, u, slot):
        piece = rsbuf.at[n, u, slot]
        remote(piece, piece, rs_send.at[n, u], rs_recv.at[n, u, slot], on_ring(1)).wait_recv()

    def reduce_far(n, u):
        reduce_send(n, u, block(u, 4), 1, 2)
        reduce_send(n, u, block(u, 3), 0, 1)
        reduce_send(n, u, block(u, 5), 2, -1)

    def reduce_near(n, u):
        reduce_send(n, u, block(u, 1), 3, 1)
        reduce_send(n, u, block(u, 7), 4, -1)

    def reduce_relay(n, u):
        reduce_wait(n, u, 0)
        reduce_wait(n, u, 1)
        block(u, 2)[...] = block(u, 2)[...] + rsbuf[n, u, 0] + rsbuf[n, u, 1]
        reduce_send(n, u, block(u, 2), 5, 2)
        reduce_wait(n, u, 2)
        block(u, 6)[...] = block(u, 6)[...] + rsbuf[n, u, 2]
        reduce_send(n, u, block(u, 6), 6, -2)

    def reduce_final(n, u):
        reduce_wait(n, u, 3)
        reduce_wait(n, u, 4)
        total = block(u, 0)[...] + rsbuf[n, u, 3] + rsbuf[n, u, 4]
        reduce_wait(n, u, 5)
        reduce_wait(n, u, 6)
        return total + rsbuf[n, u, 5] + rsbuf[n, u, 6]

    def reduce_sent(n, u):
        seven = rsbuf.at[n, u]
        remote(seven, seven, rs_send.at[n, u], rs_recv.at[n, u, 0], other).wait_send()

    def own_image(n, u, vector):
        cols = slice(u * TILE, (u + 1) * TILE)
        turned[n + 1, 0, u, own_rows] = live[:, cols] * (
            reduce_final(n, u) + site[:, cols] * vector)

    def carry(q, cols):
        a, b = rhi[q, 0, :, cols], rhi[q, 1, :, cols]
        acc = (dot(vhi[0], a) + dot(vhi[1], b) + dot(vlo[0], a) + dot(vlo[1], b)
               + dot(vhi[0], rlo[q, 0, :, cols]) + dot(vhi[1], rlo[q, 1, :, cols]))
        chi[q, :, cols], clo[q, :, cols] = split(acc)

    def bring_back(rows, cols):
        terms = [
            dot(lhi[q, rows], chi[q, :, cols]) + dot(llo[q, rows], chi[q, :, cols])
            + dot(lhi[q, rows], clo[q, :, cols])
            for q in range(4)
        ]
        return (terms[0] + terms[1]) + (terms[2] + terms[3])

    far_rows, near_rows = slice(0, HALF), slice(HALF, PAD)
    every = slice(0, HALF)

    def operate(after_far):
        for q in range(4):
            carry(q, every)
        for rows, then in ((far_rows, after_far), (near_rows, None)):
            fresh = bring_back(rows, every)
            for u in range(2):
                part[u, rows] = fresh[:, u * TILE:(u + 1) * TILE]
            if then is not None:
                then()

    CHUNK = 128

    def over_chunks(body, sums):
        totals = [[], []]
        for half in range(2):
            def step(i, acc, half=half):
                rows = pl.ds(pl.multiple_of(i * CHUNK, CHUNK), CHUNK)
                for u in range(2):
                    values = body(half, u, rows)
                    acc = tuple(
                        a + jnp.sum(v.reshape(CHUNK // 8, 8, TILE), axis=0)
                        for a, v in zip(acc, values))
                return acc
            zero = tuple(jnp.zeros((8, TILE), F32) for _ in range(sums))
            acc = lax.fori_loop(0, PAD // CHUNK, step, zero)
            totals[half] = [jnp.sum(a, axis=(0, 1), keepdims=True) for a in acc]
        return [a + b for a, b in zip(*totals)]

    def store_split(half, u, rows, value):
        hi, lo = split(value)
        vhi[half, rows, pl.ds(u * TILE, TILE)] = hi
        vlo[half, rows, pl.ds(u * TILE, TILE)] = lo

    for cp in inputs:
        cp.wait_send()
    inputs_in = [
        remote(buf.at[peer_rows], buf.at[peer_rows], insend.at[k], inrecv.at[k], other)
        for k, buf in enumerate((start, site))
    ]
    for cp in inputs_in:
        cp.wait_recv()
    start[my_rows] = init_ref[:, own_cols]
    site[my_rows] = site_ref[:, own_cols]
    masked = live * start[...]
    phases = []
    for u in range(2):
        turned[0, 0, u, own_rows] = masked[:, u * TILE:(u + 1) * TILE]
        phases.append(gather_start(0, u))
    for forward, _ in phases:
        forward()
    for _, finish in phases:
        finish()

    def first_split(half, u, rows):
        value = turned[0, half, u, rows]
        store_split(half, u, rows, value)
        return (value * value,)

    (norm_square,) = over_chunks(first_split, 1)

    for j in range(2):
        local_left[j].wait()
        left_cross[j].wait()
    for q in range(4):
        for k in range(RING):
            hi, lo = split(lstage[q, rows_of(chip(k + 2))])
            lhi[q, pl.ds(k * ROWS, ROWS)] = hi
            llo[q, pl.ds(k * ROWS, ROWS)] = lo

    present = jnp.where(s + 1 < SECTIONS, 1.0, 0.0).astype(F32)

    def diag_arrived(q, piece):
        width = HALF - piece * TILE
        ref = rdiag.at[q, pl.ds(piece * TILE, TILE), pl.ds(piece * TILE, width)]
        remote(ref, ref, rsend.at[0, 0], drecv.at[q, piece], other).wait_recv()

    def off_arrived(q, piece):
        ref = off_piece(q, piece)
        remote(ref, ref, rsend.at[0, 0], brecv.at[q, piece], other).wait_recv()

    def put(q, half, rows, cols, value):
        hi, lo = split(value * present)
        rhi[q, half, rows, cols] = hi
        rlo[q, half, rows, cols] = lo

    low, high = slice(0, TILE), slice(TILE, HALF)

    def prepare(q, u):
        diag_arrived(q, u)
        if u == 0:
            put(q, 0, low, every, rdiag[q, low, :])
            put(q, 0, high, low, rdiag[q, low, high].T)

            @pl.when(c == 0)
            def _():
                put(q, 1, every, low, roff[q, low, :].T)

            @pl.when(c == 1)
            def _():
                put(q, 1, every, low, roff[q, :, low])
        else:
            put(q, 0, high, high, rdiag[q, high, high])

            @pl.when(c == 0)
            def _():
                put(q, 1, every, high, roff[q, high, :].T)

            @pl.when(c == 1)
            def _():
                put(q, 1, every, high, roff[q, :, high])

    subs = (low, high)
    forwards = []
    first_gather = []
    for u in range(2):
        for j in range(2):
            pieces = (0, 1) if u == 0 else (2,)
            for piece in pieces:
                off_arrived(2 * j, piece)
                forwards.append(off_forward(j, piece))
                forwards[-1].start()
            prepare(2 * j, u)
            carry(2 * j, subs[u])
            for piece in pieces:
                off_arrived(2 * j + 1, piece)
            prepare(2 * j + 1, u)
            carry(2 * j + 1, subs[u])
        part[u, far_rows] = bring_back(far_rows, subs[u])
        reduce_far(0, u)
        part[u, near_rows] = bring_back(near_rows, subs[u])
        reduce_near(0, u)
        if u == 1:
            first_gather[0][0]()
        reduce_relay(0, u)
        if u == 1:
            first_gather[0][1]()
        own_image(0, u, turned[0, 0, u, own_rows])
        first_gather.append(gather_start(1, u))
    first_gather[1][0]()
    first_gather[1][1]()
    for cp in shifts + forwards:
        cp.wait_send()
    for u in range(2):
        reduce_sent(0, u)

    inverse = 1.0 / jnp.sqrt(norm_square)

    def first_ritz(half, u, rows):
        est = turned[0, half, u, rows] * inverse
        img = turned[1, half, u, rows] * inverse
        estimate[half, u, rows] = est
        image[half, u, rows] = img
        return (est * img,)

    (ritz,) = over_chunks(first_ritz, 1)

    def first_residual(half, u, rows):
        res = image[half, u, rows] - ritz * estimate[half, u, rows]
        resid[half, u, rows] = res
        store_split(half, u, rows, res)
        return (res * res,)

    (res_square,) = over_chunks(first_residual, 1)

    def coefficients(ritz, res_square, bend):
        half_gap = 0.5 * (bend - ritz)
        radius = jnp.sqrt(half_gap * half_gap + res_square)
        step = -jnp.sqrt(res_square) / (half_gap + radius)
        back = 1.0 / jnp.sqrt(1.0 + step * step)
        return step, back, ritz + half_gap - radius

    def iterate(n, carried):
        ritz, res_square = carried

        def send_far():
            for u in range(2):
                reduce_far(n, u)

        operate(send_far)
        for u in range(2):
            reduce_near(n, u)
        for u in range(2):
            reduce_relay(n, u)
        phases = []
        for u in range(2):
            own_image(n, u, resid[0, u, own_rows])
            phases.append(gather_start(n + 1, u))
        for forward, _ in phases:
            forward()
        for _, finish in phases:
            finish()
        for u in range(2):
            reduce_sent(n, u)
        inverse = 1.0 / jnp.sqrt(res_square)

        def bends(half, u, rows):
            return ((resid[half, u, rows] * inverse) * (turned[n + 1, half, u, rows] * inverse),)

        (bend,) = over_chunks(bends, 1)
        step, back, new_ritz = coefficients(ritz, res_square, bend)
        scaled = step * inverse

        def update(half, u, rows):
            est = (estimate[half, u, rows] + scaled * resid[half, u, rows]) * back
            img = (image[half, u, rows] + scaled * turned[n + 1, half, u, rows]) * back
            estimate[half, u, rows] = est
            image[half, u, rows] = img
            res = img - new_ritz * est
            resid[half, u, rows] = res
            store_split(half, u, rows, res)
            return (res * res,)

        (new_square,) = over_chunks(update, 1)
        return new_ritz, new_square

    ritz, res_square = lax.fori_loop(1, ITERS, iterate, (ritz, res_square))

    operate(None)
    inverse = 1.0 / jnp.sqrt(res_square)
    mine = []
    for u in range(2):
        own = resid[0, u, own_rows] * inverse
        acc = site[:, subs[u]] * own * own
        for k in range(RING):
            acc = acc + (block(u, k)[...] * inverse) * (resid[0, u, rows_of(chip(k))] * inverse)
        mine.append(jnp.sum(acc, axis=(0, 1), keepdims=True))
    mine = mine[0] + mine[1]
    scal[t] = jnp.broadcast_to(mine, (8, 128))
    bends = []
    for k in range(1, 2 * RING):
        cp = remote(scal.at[t], scal.at[t], sc_send.at[k], sc_recv.at[k],
                    (s, lax.rem(t + k, 2 * RING)))
        cp.start()
        bends.append(cp)
    for k in range(1, 2 * RING):
        slot = scal.at[lax.rem(t + 2 * RING - k, 2 * RING)]
        remote(slot, slot, sc_send.at[k], sc_recv.at[k], other).wait_recv()
    bend = jnp.sum(scal[...], axis=0)[0:1, 0:1]
    step, back, ritz = coefficients(ritz, res_square, bend)
    scaled = step * inverse
    out_rows = pl.ds(pl.multiple_of(t * (ROWS // 2), ROWS // 2), ROWS // 2)
    for half, base in ((0, c * HALF), (1, (1 - c) * HALF)):
        for u in range(2):
            est = (estimate[half, u, out_rows] + scaled * resid[half, u, out_rows]) * back
            cols = pl.ds(pl.multiple_of(base + u * TILE, TILE), TILE)
            out_ref[:, cols] = est * (0.5 * PAD)
    energy_ref[0] = ritz[0, 0]
    for cp in bends:
        cp.wait_send()
    for n in range(ITERS + 1):
        for u in range(2):
            gather_sent(n, u)


def per_device(initial, onsite, left_env, right_env, sector_dims):
    vmem = pl.BlockSpec(memory_space=pltpu.VMEM)
    smem = pl.BlockSpec(memory_space=pltpu.SMEM)
    anywhere = pl.BlockSpec(memory_space=pl.ANY)
    dma = pltpu.SemaphoreType.DMA
    full = (2, 2, PAD, TILE)
    return pl.pallas_call(
        kernel,
        out_shape=(
            jax.ShapeDtypeStruct((ROWS // 2, PAD), F32),
            jax.ShapeDtypeStruct((1,), F32),
        ),
        in_specs=[vmem, vmem, anywhere, anywhere, smem],
        out_specs=(vmem, smem),
        scratch_shapes=[
            pltpu.VMEM((4, PAD, PAD), F32),
            pltpu.VMEM((4, PAD, PAD), BF16),
            pltpu.VMEM((4, PAD, PAD), BF16),
            pltpu.VMEM((4, HALF, HALF), F32),
            pltpu.VMEM((4, HALF, HALF), F32),
            pltpu.VMEM((4, 2, HALF, HALF), BF16),
            pltpu.VMEM((4, 2, HALF, HALF), BF16),
            pltpu.VMEM((4, PAD, HALF), BF16),
            pltpu.VMEM((4, PAD, HALF), BF16),
            pltpu.VMEM((ROWS, HALF), F32),
            pltpu.VMEM((ROWS, HALF), F32),
            pltpu.VMEM((ITERS + 1,) + full, F32),
            pltpu.VMEM(full, F32),
            pltpu.VMEM(full, F32),
            pltpu.VMEM(full, F32),
            pltpu.VMEM((2, PAD, HALF), BF16),
            pltpu.VMEM((2, PAD, HALF), BF16),
            pltpu.VMEM((2, PAD, TILE), F32),
            pltpu.VMEM((ITERS, 2, 7, ROWS, TILE), F32),
            pltpu.VMEM((2 * RING, 8, 128), F32),
            dma((2,)), dma((2,)), dma((2,)), dma((2,)), dma((2,)),
            dma((2, 7)), dma((4, 2)), dma((4, 3)), dma((2, 3)),
            dma((ITERS, 2)), dma((ITERS, 2, 7)),
            dma((ITERS + 1, 2)), dma((ITERS + 1, 2, 7)),
            dma((ITERS + 1, 2)), dma((ITERS + 1, 2)),
            dma((2 * RING,)), dma((2 * RING,)),
        ],
        compiler_params=pltpu.CompilerParams(
            collective_id=0, has_side_effects=True, vmem_limit_bytes=56 * 2**20),
        cost_estimate=pl.CostEstimate(
            flops=5 * 3 * 2 * 4 * 2 * PAD * PAD * HALF, bytes_accessed=2**23, transcendentals=0),
    )(initial, onsite, left_env, right_env, sector_dims)


def solution(mesh):
    return jax.shard_map(
        per_device,
        mesh=mesh,
        in_specs=(
            P(("sec", "term"), None),
            P(("sec", "term"), None),
            P("sec", "term", None, None),
            P("sec", "term", None, None),
            P("sec", None),
        ),
        out_specs=(P(("sec", "term"), None), P("sec")),
        check_vma=False,
    )
```

```python
import functools

import jax
import jax.numpy as jnp
from jax import lax
from jax.experimental import pallas as pl
from jax.experimental.pallas import tpu as pltpu
from jax.sharding import PartitionSpec as P

ITERS = 4
PAD = 512
HALF = 256
TILE = 128
RING = 8
SECTIONS = 16
ROWS = PAD // RING
MESH = pl.DeviceIdType.MESH
F32, BF16 = jnp.float32, jnp.bfloat16


def dot(a, b):
    return jnp.dot(a, b, preferred_element_type=F32)


def split(x):
    high = x.astype(BF16)
    return high, (x - high.astype(F32)).astype(BF16)


def kernel(
    init_ref, site_ref, left_ref, right_ref, dims_ref, out_ref, energy_ref,
    lstage, lhi, llo, tiles, packed_out, packed, corner, roff, rhi, rlo, chi, clo, cacc,
    start, site, turned, estimate, image, resid, vhi, vlo, part, rsbuf, scal,
    lsem, tsem, lsend, lrecv, insend, inrecv, rsend, psend, precv, drecv, brecv, bfwd,
    rs_send, rs_recv, ag_send, ag_recv, cross_send, cross_recv, sc_send, sc_recv,
):
    s, t = lax.axis_index("sec"), lax.axis_index("term")
    z, c = t // 2, t % 2
    sign = 2 * c - 1

    def chip(k):
        return lax.rem(z + sign * k + 2 * RING, RING)

    def on_ring(k):
        return (s, chip(k) * 2 + c)

    other = (s, z * 2 + 1 - c)
    before = lax.rem(s + SECTIONS - 1, SECTIONS)
    after = lax.rem(s + 1, SECTIONS)

    def rows_of(chip_index):
        return pl.ds(pl.multiple_of(chip_index * ROWS, ROWS), ROWS)

    def remote(src, dst, send, recv, to):
        return pltpu.make_async_remote_copy(
            src_ref=src, dst_ref=dst, send_sem=send, recv_sem=recv,
            device_id=to, device_id_type=MESH,
        )

    local_left = [
        pltpu.make_async_copy(left_ref.at[0, j], lstage.at[2 * j], lsem.at[j])
        for j in range(2)
    ]
    for cp in local_left:
        cp.start()

    def tile_copy(j, kind, u):
        base = pl.multiple_of((c if kind == 0 else 1 - c) * HALF + u * TILE, TILE)
        return pltpu.make_async_copy(
            right_ref.at[0, j, pl.ds(base, TILE), pl.ds(base, TILE)],
            tiles.at[j, kind, u], tsem.at[j, kind, u])

    for u in range(2):
        for kind in range(2):
            for j in range(2):
                tile_copy(j, kind, u).start()

    barrier = pltpu.get_barrier_semaphore()
    greeted = [on_ring(k) for k in (1, -1, 2, -2)] + [other]
    greeted += [(after, z * 2 + k) for k in range(2)]
    for device in greeted:
        pl.semaphore_signal(barrier, inc=1, device_id=device, device_id_type=MESH)
    pl.semaphore_wait(barrier, len(greeted))

    own_cols = pl.ds(pl.multiple_of(c * HALF, HALF), HALF)
    other_cols = pl.ds(pl.multiple_of((1 - c) * HALF, HALF), HALF)
    my_rows = pl.ds(pl.multiple_of(c * (ROWS // 2), ROWS // 2), ROWS // 2)
    peer_rows = pl.ds(pl.multiple_of((1 - c) * (ROWS // 2), ROWS // 2), ROWS // 2)
    inputs = [
        remote(ref.at[:, other_cols], buf.at[my_rows], insend.at[k], inrecv.at[k], other)
        for k, (ref, buf) in enumerate(((init_ref, start), (site_ref, site)))
    ]
    for cp in inputs:
        cp.start()

    def target(kind):
        return (before, z * 2 + (c if kind == 0 else 1 - c))

    def corner_copy(j, kind):
        base = (c if kind == 0 else 1 - c) * HALF
        return remote(
            right_ref.at[0, j, pl.ds(pl.multiple_of(base, TILE), TILE),
                         pl.ds(pl.multiple_of(base + TILE, TILE), TILE)],
            corner.at[2 * j + kind], rsend.at[j, kind], drecv.at[2 * j + kind], target(kind))

    off_parts = ((0, 0, HALF), (TILE, 0, TILE), (TILE, TILE, TILE))

    def off_piece(slot, piece):
        r0, c0, width = off_parts[piece]
        return roff.at[slot, pl.ds(r0, TILE), pl.ds(c0, width)]

    def off_copy(j, piece):
        r0, c0, width = off_parts[piece]
        return remote(
            right_ref.at[0, j, pl.ds(r0, TILE), pl.ds(HALF + c0, width)],
            off_piece(2 * j, piece), rsend.at[j, 2 + piece], brecv.at[2 * j, piece],
            (before, t))

    def off_forward(j, piece):
        return remote(off_piece(2 * j, piece), off_piece(2 * j + 1, piece),
                      bfwd.at[j, piece], brecv.at[2 * j + 1, piece], other)

    def packed_copy(kind, u):
        return remote(packed_out.at[kind, u], packed.at[kind, u],
                      psend.at[kind, u], precv.at[kind, u], target(kind))

    tile_row = lax.broadcasted_iota(jnp.int32, (TILE, TILE), 0)
    tile_col = lax.broadcasted_iota(jnp.int32, (TILE, TILE), 1)

    def pack(kind, u):
        for j in range(2):
            tile_copy(j, kind, u).wait()
        second = tiles[1, kind, u]
        packed_out[kind, u, pl.ds(0, TILE)] = jnp.where(
            tile_row <= tile_col, tiles[0, kind, u], second)
        line = jnp.sum(jnp.where(tile_row == tile_col, second, 0.0), axis=0, keepdims=True)
        packed_out[kind, u, pl.ds(TILE, 8)] = jnp.broadcast_to(line, (8, TILE))

    def unpack(kind, u):
        both = packed[kind, u, pl.ds(0, TILE)]
        line = packed[kind, u, pl.ds(TILE, 8)][0:1]
        mirrored = both.T
        first = jnp.where(tile_row <= tile_col, both, mirrored)
        second = jnp.where(tile_row > tile_col, both, mirrored)
        return first, jnp.where(tile_row == tile_col, line, second)

    shifts = [off_copy(0, 0), off_copy(0, 1), corner_copy(0, 0), corner_copy(0, 1)]
    for cp in shifts:
        cp.start()
    for u in range(2):
        for kind in range(2):
            pack(kind, u)
    later = [packed_copy(0, 0), packed_copy(1, 0)]
    later += [off_copy(1, 0), off_copy(1, 1), corner_copy(1, 0), corner_copy(1, 1)]
    later += [packed_copy(0, 1), packed_copy(1, 1), off_copy(0, 2), off_copy(1, 2)]
    for cp in later:
        cp.start()
    shifts += later
    left_cross = [
        remote(left_ref.at[0, j], lstage.at[2 * j + 1], lsend.at[j], lrecv.at[j], other)
        for j in range(2)
    ]
    for cp in left_cross:
        cp.start()

    row_index = lax.broadcasted_iota(jnp.int32, (ROWS, HALF), 0) + z * ROWS
    col_index = lax.broadcasted_iota(jnp.int32, (ROWS, HALF), 1) + c * HALF
    live = jnp.where(
        (row_index < dims_ref[0, 0]) & (col_index < dims_ref[0, 1]), 1.0, 0.0).astype(F32)

    own_rows = rows_of(z)

    def gather_start(n, u):
        def ring_copy(k, src_chip, index):
            piece = turned.at[n, 0, u, rows_of(src_chip)]
            return remote(piece, piece, ag_send.at[n, u], ag_recv.at[n, u, index], on_ring(k))

        def cross(k):
            rows = rows_of(chip(k))
            remote(turned.at[n, 0, u, rows], turned.at[n, 1, u, rows],
                   cross_send.at[n, u], cross_recv.at[n, u], other).start()

        def received(index, k):
            piece = turned.at[n, 0, u, rows_of(chip(k))]
            remote(piece, piece, ag_send.at[n, u], ag_recv.at[n, u, index],
                   on_ring(k)).wait_recv()

        ring_copy(2, z, 0).start()
        ring_copy(-2, z, 1).start()
        ring_copy(1, z, 2).start()
        ring_copy(-1, z, 3).start()
        cross(0)

        def forward():
            received(0, -2)
            ring_copy(2, chip(-2), 5).start()
            ring_copy(1, chip(-2), 4).start()
            received(1, 2)
            ring_copy(-1, chip(2), 6).start()
            cross(-2)
            cross(2)
            received(2, -1)
            cross(-1)
            received(3, 1)
            cross(1)

        def finish():
            received(4, -3)
            cross(-3)
            received(6, 3)
            cross(3)
            received(5, -4)
            cross(-4)

        def complete():
            other_half = turned.at[n, 1, u]
            remote(other_half, other_half, cross_send.at[n, u], cross_recv.at[n, u],
                   other).wait_recv()

        return forward, finish, complete

    def gather_sent(n, u):
        seven = rsbuf.at[0, 0]
        remote(seven, seven, ag_send.at[n, u], ag_recv.at[n, u, 0], other).wait_send()
        half = turned.at[n, 0, u]
        remote(half, half, cross_send.at[n, u], cross_recv.at[n, u], other).wait_send()

    def block(u, j):
        return part.at[u, pl.ds((j + 6) % RING * ROWS, ROWS)]

    def reduce_send(n, u, src, slot, k):
        remote(src, rsbuf.at[n, u, slot], rs_send.at[n, u], rs_recv.at[n, u, slot],
               on_ring(k)).start()

    def reduce_wait(n, u, slot):
        piece = rsbuf.at[n, u, slot]
        remote(piece, piece, rs_send.at[n, u], rs_recv.at[n, u, slot], on_ring(1)).wait_recv()

    def reduce_far(n, u):
        reduce_send(n, u, block(u, 4), 1, 2)
        reduce_send(n, u, block(u, 3), 0, 1)
        reduce_send(n, u, block(u, 5), 2, -1)

    def reduce_near(n, u):
        reduce_send(n, u, block(u, 1), 3, 1)
        reduce_send(n, u, block(u, 7), 4, -1)

    def reduce_relay(n, u):
        reduce_wait(n, u, 0)
        reduce_wait(n, u, 1)
        block(u, 2)[...] = block(u, 2)[...] + rsbuf[n, u, 0] + rsbuf[n, u, 1]
        reduce_send(n, u, block(u, 2), 5, 2)
        reduce_wait(n, u, 2)
        block(u, 6)[...] = block(u, 6)[...] + rsbuf[n, u, 2]
        reduce_send(n, u, block(u, 6), 6, -2)

    def reduce_final(n, u):
        reduce_wait(n, u, 3)
        reduce_wait(n, u, 4)
        total = block(u, 0)[...] + rsbuf[n, u, 3] + rsbuf[n, u, 4]
        reduce_wait(n, u, 5)
        reduce_wait(n, u, 6)
        return total + rsbuf[n, u, 5] + rsbuf[n, u, 6]

    def reduce_sent(n, u):
        seven = rsbuf.at[n, u]
        remote(seven, seven, rs_send.at[n, u], rs_recv.at[n, u, 0], other).wait_send()

    def own_image(n, u, vector):
        cols = slice(u * TILE, (u + 1) * TILE)
        turned[n + 1, 0, u, own_rows] = live[:, cols] * (
            reduce_final(n, u) + site[:, cols] * vector)

    def carry(q, u):
        cols = slice(u * TILE, (u + 1) * TILE)
        acc = None
        for k in range(2):
            new = (dot(vhi[k], rhi[q, k, :, cols]) + dot(vlo[k], rhi[q, k, :, cols])
                   + dot(vhi[k], rlo[q, k, :, cols]))
            acc = new if acc is None else acc + new
        chi[q, :, cols], clo[q, :, cols] = split(acc)

    def carry_part(q, k):
        return dot(vhi[k], rhi[q, k]) + dot(vlo[k], rhi[q, k]) + dot(vhi[k], rlo[q, k])

    def bring_back(rows, cols):
        terms = [
            dot(lhi[q, rows], chi[q, :, cols]) + dot(llo[q, rows], chi[q, :, cols])
            + dot(lhi[q, rows], clo[q, :, cols])
            for q in range(4)
        ]
        return (terms[0] + terms[1]) + (terms[2] + terms[3])

    far_rows, near_rows = slice(0, HALF), slice(HALF, PAD)
    every = slice(0, HALF)

    def products(u):
        cols = slice(u * TILE, (u + 1) * TILE)
        part[u, far_rows] = bring_back(far_rows, cols)
        reduce_far(0, u)
        part[u, near_rows] = bring_back(near_rows, cols)
        reduce_near(0, u)

    def operate(after_far):
        for rows, then in ((far_rows, after_far), (near_rows, None)):
            fresh = bring_back(rows, every)
            for u in range(2):
                part[u, rows] = fresh[:, u * TILE:(u + 1) * TILE]
            if then is not None:
                then()

    CHUNK = 128

    def over_chunks(body, u):
        totals = []
        for half in range(2):
            def step(i, acc, half=half):
                value = body(half, u, pl.ds(pl.multiple_of(i * CHUNK, CHUNK), CHUNK))
                return acc + jnp.sum(value.reshape(CHUNK // 8, 8, TILE), axis=0)
            acc = lax.fori_loop(0, PAD // CHUNK, step, jnp.zeros((8, TILE), F32))
            totals.append(jnp.sum(acc, axis=(0, 1), keepdims=True))
        return totals

    def combine(first, second):
        return (first[0] + second[0]) + (first[1] + second[1])

    def store_split(half, u, rows, value):
        hi, lo = split(value)
        vhi[u, rows, pl.ds(half * TILE, TILE)] = hi
        vlo[u, rows, pl.ds(half * TILE, TILE)] = lo

    def bend_part(u, inverse):
        own = resid[0, u, own_rows] * inverse
        acc = site[:, u * TILE:(u + 1) * TILE] * own * own
        for k in range(RING):
            acc = acc + (block(u, k)[...] * inverse) * (
                resid[0, u, rows_of(chip(k))] * inverse)
        return jnp.sum(acc, axis=(0, 1), keepdims=True)

    def send_bend(n, mine):
        scal[n, t] = jnp.broadcast_to(mine, (1, TILE))
        for k in range(1, 2 * RING):
            remote(scal.at[n, t], scal.at[n, t], sc_send.at[n], sc_recv.at[n],
                   (s, lax.rem(t + k, 2 * RING))).start()

    def bend_total(n):
        others = scal.at[n, pl.ds(0, 2 * RING - 1)]
        remote(others, others, sc_send.at[n], sc_recv.at[n], other).wait()
        return jnp.sum(scal[n], axis=0)[:, 0:1]

    def coefficients(ritz, res_square, bend):
        half_gap = 0.5 * (bend - ritz)
        radius = jnp.sqrt(half_gap * half_gap + res_square)
        step = -jnp.sqrt(res_square) / (half_gap + radius)
        back = 1.0 / jnp.sqrt(1.0 + step * step)
        return step, back, ritz + half_gap - radius

    def absorb(n, u, scaled, back, ritz):
        def update(half, u, rows):
            est = (estimate[half, u, rows] + scaled * resid[half, u, rows]) * back
            img = (image[half, u, rows] + scaled * turned[n + 1, half, u, rows]) * back
            estimate[half, u, rows] = est
            image[half, u, rows] = img
            res = img - ritz * est
            resid[half, u, rows] = res
            store_split(half, u, rows, res)
            return res * res

        sums = over_chunks(update, u)
        for q in range(4):
            if u == 0:
                cacc[q] = carry_part(q, 0)
            else:
                chi[q], clo[q] = split(cacc[q] + carry_part(q, 1))
        return sums

    def take_in(n, phases, scaled, back, ritz):
        phases[0][1]()
        phases[0][2]()
        first = absorb(n, 0, scaled, back, ritz)
        phases[1][1]()
        phases[1][2]()
        second = absorb(n, 1, scaled, back, ritz)
        return combine(first, second)

    for cp in inputs:
        cp.wait_send()
    inputs_in = [
        remote(buf.at[peer_rows], buf.at[peer_rows], insend.at[k], inrecv.at[k], other)
        for k, buf in enumerate((start, site))
    ]
    for cp in inputs_in:
        cp.wait_recv()
    start[my_rows] = init_ref[:, own_cols]
    site[my_rows] = site_ref[:, own_cols]
    masked = live * start[...]
    phases = []
    for u in range(2):
        turned[0, 0, u, own_rows] = masked[:, u * TILE:(u + 1) * TILE]
        phases.append(gather_start(0, u))
    for forward, _, _ in phases:
        forward()
    for _, finish, complete in phases:
        finish()
        complete()

    def first_split(half, u, rows):
        value = turned[0, half, u, rows]
        zero = jnp.zeros_like(value)
        resid[half, u, rows] = value
        estimate[half, u, rows] = zero
        image[half, u, rows] = zero
        store_split(half, u, rows, value)
        return value * value

    norm_square = combine(over_chunks(first_split, 0), over_chunks(first_split, 1))

    for j in range(2):
        local_left[j].wait()
        left_cross[j].wait()
    for q in range(4):
        for k in range(RING):
            hi, lo = split(lstage[q, rows_of(chip(k + 2))])
            lhi[q, pl.ds(k * ROWS, ROWS)] = hi
            llo[q, pl.ds(k * ROWS, ROWS)] = lo

    present = jnp.where(s + 1 < SECTIONS, 1.0, 0.0).astype(F32)

    def arrived(ref, sem):
        remote(ref, ref, rsend.at[0, 0], sem, other).wait_recv()

    def put(q, k, half, u, value):
        hi, lo = split(value * present)
        rows, cols = pl.ds(half * TILE, TILE), pl.ds(u * TILE, TILE)
        rhi[q, k, rows, cols] = hi
        rlo[q, k, rows, cols] = lo

    def put_off(q, u):
        for k in range(2):
            @pl.when(c == 0)
            def _():
                put(q, k, 1, u, roff[q, pl.ds(u * TILE, TILE), pl.ds(k * TILE, TILE)].T)

            @pl.when(c == 1)
            def _():
                put(q, k, 1, u, roff[q, pl.ds(k * TILE, TILE), pl.ds(u * TILE, TILE)])

    def put_diag(u):
        for kind in range(2):
            arrived(packed.at[kind, u], precv.at[kind, u])
            for j, value in enumerate(unpack(kind, u)):
                put(2 * j + kind, u, 0, u, value)

    forwards = []

    def off_arrived(j, u):
        for piece in ((0, 1) if u == 0 else (2,)):
            arrived(off_piece(2 * j, piece), brecv.at[2 * j, piece])
            forwards.append(off_forward(j, piece))
            forwards[-1].start()

    def first_carry(j, u):
        for q in (2 * j, 2 * j + 1):
            if q % 2:
                for piece in ((0, 1) if u == 0 else (2,)):
                    arrived(off_piece(q, piece), brecv.at[q, piece])
            put_off(q, u)
            if u == 0:
                arrived(corner.at[q], drecv.at[q])
                put(q, 0, 0, 1, corner[q])
                put(q, 1, 0, 0, corner[q].T)
            carry(q, u)

    off_arrived(0, 0)
    put_diag(0)
    first_carry(0, 0)
    off_arrived(1, 0)
    first_carry(1, 0)
    products(0)
    inverse = 1.0 / jnp.sqrt(norm_square)
    bend_share = bend_part(0, inverse)
    off_arrived(0, 1)
    put_diag(1)
    first_carry(0, 1)
    reduce_relay(0, 0)
    off_arrived(1, 1)
    first_carry(1, 1)
    own_image(0, 0, resid[0, 0, own_rows])
    phases = [gather_start(1, 0)]
    products(1)
    send_bend(0, bend_share + bend_part(1, inverse))
    phases[0][0]()
    reduce_relay(0, 1)
    own_image(0, 1, resid[0, 1, own_rows])
    phases.append(gather_start(1, 1))
    ritz = bend_total(0)
    phases[1][0]()
    res_square = take_in(0, phases, inverse, 1.0, ritz)
    for cp in shifts + forwards:
        cp.wait_send()
    for u in range(2):
        reduce_sent(0, u)

    def iterate(n, carried):
        ritz, res_square = carried
        inverse = 1.0 / jnp.sqrt(res_square)

        def send_far():
            for u in range(2):
                reduce_far(n, u)

        operate(send_far)
        for u in range(2):
            reduce_near(n, u)
        send_bend(n, bend_part(0, inverse) + bend_part(1, inverse))
        for u in range(2):
            reduce_relay(n, u)
        phases = []
        for u in range(2):
            own_image(n, u, resid[0, u, own_rows])
            phases.append(gather_start(n + 1, u))
        step, back, new_ritz = coefficients(ritz, res_square, bend_total(n))
        for forward, _, _ in phases:
            forward()
        new_square = take_in(n, phases, step * inverse, back, new_ritz)
        for u in range(2):
            reduce_sent(n, u)
        return new_ritz, new_square

    ritz, res_square = lax.fori_loop(1, ITERS, iterate, (ritz, res_square))

    operate(None)
    inverse = 1.0 / jnp.sqrt(res_square)
    send_bend(ITERS, bend_part(0, inverse) + bend_part(1, inverse))
    step, back, ritz = coefficients(ritz, res_square, bend_total(ITERS))
    scaled = step * inverse
    out_rows = pl.ds(pl.multiple_of(t * (ROWS // 2), ROWS // 2), ROWS // 2)
    for half, base in ((0, c * HALF), (1, (1 - c) * HALF)):
        for u in range(2):
            est = (estimate[half, u, out_rows] + scaled * resid[half, u, out_rows]) * back
            cols = pl.ds(pl.multiple_of(base + u * TILE, TILE), TILE)
            out_ref[:, cols] = est * (0.5 * PAD)
    energy_ref[0] = ritz[0, 0]
    for n in range(ITERS + 1):
        for u in range(2):
            gather_sent(n, u)


def per_device(initial, onsite, left_env, right_env, sector_dims):
    vmem = pl.BlockSpec(memory_space=pltpu.VMEM)
    smem = pl.BlockSpec(memory_space=pltpu.SMEM)
    anywhere = pl.BlockSpec(memory_space=pl.ANY)
    dma = pltpu.SemaphoreType.DMA
    full = (2, 2, PAD, TILE)
    return pl.pallas_call(
        kernel,
        out_shape=(
            jax.ShapeDtypeStruct((ROWS // 2, PAD), F32),
            jax.ShapeDtypeStruct((1,), F32),
        ),
        in_specs=[vmem, vmem, anywhere, anywhere, smem],
        out_specs=(vmem, smem),
        scratch_shapes=[
            pltpu.VMEM((4, PAD, PAD), F32),
            pltpu.VMEM((4, PAD, PAD), BF16),
            pltpu.VMEM((4, PAD, PAD), BF16),
            pltpu.VMEM((2, 2, 2, TILE, TILE), F32),
            pltpu.VMEM((2, 2, TILE + 8, TILE), F32),
            pltpu.VMEM((2, 2, TILE + 8, TILE), F32),
            pltpu.VMEM((4, TILE, TILE), F32),
            pltpu.VMEM((4, HALF, HALF), F32),
            pltpu.VMEM((4, 2, HALF, HALF), BF16),
            pltpu.VMEM((4, 2, HALF, HALF), BF16),
            pltpu.VMEM((4, PAD, HALF), BF16),
            pltpu.VMEM((4, PAD, HALF), BF16),
            pltpu.VMEM((4, PAD, HALF), F32),
            pltpu.VMEM((ROWS, HALF), F32),
            pltpu.VMEM((ROWS, HALF), F32),
            pltpu.VMEM((ITERS + 1,) + full, F32),
            pltpu.VMEM(full, F32),
            pltpu.VMEM(full, F32),
            pltpu.VMEM(full, F32),
            pltpu.VMEM((2, PAD, HALF), BF16),
            pltpu.VMEM((2, PAD, HALF), BF16),
            pltpu.VMEM((2, PAD, TILE), F32),
            pltpu.VMEM((ITERS, 2, 7, ROWS, TILE), F32),
            pltpu.VMEM((ITERS + 1, 2 * RING, 1, TILE), F32),
            dma((2,)), dma((2, 2, 2)), dma((2,)), dma((2,)), dma((2,)), dma((2,)),
            dma((2, 5)), dma((2, 2)), dma((2, 2)), dma((4,)), dma((4, 3)), dma((2, 3)),
            dma((ITERS, 2)), dma((ITERS, 2, 7)),
            dma((ITERS + 1, 2)), dma((ITERS + 1, 2, 7)),
            dma((ITERS + 1, 2)), dma((ITERS + 1, 2)),
            dma((ITERS + 1,)), dma((ITERS + 1,)),
        ],
        compiler_params=pltpu.CompilerParams(
            collective_id=0, has_side_effects=True, vmem_limit_bytes=56 * 2**20),
        cost_estimate=pl.CostEstimate(
            flops=5 * 3 * 2 * 4 * 2 * PAD * PAD * HALF, bytes_accessed=2**23, transcendentals=0),
    )(initial, onsite, left_env, right_env, sector_dims)


def solution(mesh):
    return jax.shard_map(
        per_device,
        mesh=mesh,
        in_specs=(
            P(("sec", "term"), None),
            P(("sec", "term"), None),
            P("sec", "term", None, None),
            P("sec", "term", None, None),
            P("sec", None),
        ),
        out_specs=(P(("sec", "term"), None), P("sec")),
        check_vma=False,
    )
```

```python
import functools

import jax
import jax.numpy as jnp
from jax import lax
from jax.experimental import pallas as pl
from jax.experimental.pallas import tpu as pltpu
from jax.sharding import PartitionSpec as P

ITERS = 4
PAD = 512
HALF = 256
TILE = 128
RING = 8
SECTIONS = 16
GROUPS = ((0, -1, 1, -2, 2), (-3, 3, 4))
LONG_WAY = 3
SIDE = 4
ROWS = PAD // RING
MESH = pl.DeviceIdType.MESH
F32, BF16 = jnp.float32, jnp.bfloat16


def dot(a, b):
    return jnp.dot(a, b, preferred_element_type=F32)


def split(x):
    high = x.astype(BF16)
    return high, (x - high.astype(F32)).astype(BF16)


def kernel(
    init_ref, site_ref, left_ref, right_ref, dims_ref, out_ref, energy_ref,
    lstage, lhi, llo, tiles, packed_out, packed, corner, roff, rhi, rlo, chi, clo, squares, passing,
    start, site, turned, estimate, image, resid, vhi, vlo, part, rsbuf, scal,
    lsem, tsem, lsend, lrecv, insend, inrecv, rsend, psend, precv, drecv, brecv, bfwd, hsend, hrecv,
    rs_send, rs_recv, ag_send, ag_recv, cross_send, cross_recv, sc_send, sc_recv,
):
    s, t = lax.axis_index("sec"), lax.axis_index("term")
    z, c = t // 2, t % 2
    sign = 2 * c - 1

    def chip(k):
        return lax.rem(z + sign * k + 2 * RING, RING)

    def on_ring(k):
        return (s, chip(k) * 2 + c)

    other = (s, z * 2 + 1 - c)
    before = lax.rem(s + SECTIONS - 1, SECTIONS)
    after = lax.rem(s + 1, SECTIONS)
    x, y = s % SIDE, s // SIDE

    def section_at(x_of, y_of):
        return lax.rem(y_of + SIDE, SIDE) * SIDE + lax.rem(x_of + SIDE, SIDE)

    right, left = section_at(x + 1, y), section_at(x - 1, y)
    last_to = section_at(x + 1, y - (x == SIDE - 2).astype(jnp.int32))
    last_from = section_at(x - 1, y + (x == SIDE - 1).astype(jnp.int32))

    def rows_of(chip_index):
        return pl.ds(pl.multiple_of(chip_index * ROWS, ROWS), ROWS)

    def remote(src, dst, send, recv, to):
        return pltpu.make_async_remote_copy(
            src_ref=src, dst_ref=dst, send_sem=send, recv_sem=recv,
            device_id=to, device_id_type=MESH,
        )

    local_left = [
        pltpu.make_async_copy(left_ref.at[0, j], lstage.at[2 * j], lsem.at[j])
        for j in range(2)
    ]
    for cp in local_left:
        cp.start()

    def tile_copy(j, kind, u):
        base = pl.multiple_of((c if kind == 0 else 1 - c) * HALF + u * TILE, TILE)
        return pltpu.make_async_copy(
            right_ref.at[0, j, pl.ds(base, TILE), pl.ds(base, TILE)],
            tiles.at[j, kind, u], tsem.at[j, kind, u])

    for u in range(2):
        for kind in range(2):
            for j in range(2):
                tile_copy(j, kind, u).start()

    barrier = pltpu.get_barrier_semaphore()
    greeted = [on_ring(k) for k in (1, -1, 2, -2)] + [other]
    greeted += [(after, z * 2 + k) for k in range(2)] + [(left, t), (last_from, t)]
    for device in greeted:
        pl.semaphore_signal(barrier, inc=1, device_id=device, device_id_type=MESH)
    tile_row = lax.broadcasted_iota(jnp.int32, (TILE, TILE), 0)
    tile_col = lax.broadcasted_iota(jnp.int32, (TILE, TILE), 1)

    def pack(kind, u):
        for j in range(2):
            tile_copy(j, kind, u).wait()
        second = tiles[1, kind, u]
        packed_out[kind, u, pl.ds(0, TILE)] = jnp.where(
            tile_row <= tile_col, tiles[0, kind, u], second)
        line = jnp.sum(jnp.where(tile_row == tile_col, second, 0.0), axis=0, keepdims=True)
        packed_out[kind, u, pl.ds(TILE, 8)] = jnp.broadcast_to(line, (8, TILE))

    def split_left(q):
        for k in range(RING):
            hi, lo = split(lstage[q, rows_of(chip(k + 2))])
            lhi[q, pl.ds(k * ROWS, ROWS)] = hi
            llo[q, pl.ds(k * ROWS, ROWS)] = lo

    for u in range(2):
        for kind in range(2):
            pack(kind, u)
    for j in range(2):
        local_left[j].wait()
        split_left(2 * j)
    pl.semaphore_wait(barrier, len(greeted))

    own_cols = pl.ds(pl.multiple_of(c * HALF, HALF), HALF)
    other_cols = pl.ds(pl.multiple_of((1 - c) * HALF, HALF), HALF)
    my_rows = pl.ds(pl.multiple_of(c * (ROWS // 2), ROWS // 2), ROWS // 2)
    peer_rows = pl.ds(pl.multiple_of((1 - c) * (ROWS // 2), ROWS // 2), ROWS // 2)
    inputs = [
        remote(ref.at[:, other_cols], buf.at[my_rows], insend.at[k], inrecv.at[k], other)
        for k, (ref, buf) in enumerate(((init_ref, start), (site_ref, site)))
    ]
    for cp in inputs:
        cp.start()

    def target(kind):
        return (before, z * 2 + (c if kind == 0 else 1 - c))

    def corner_copy(j, kind):
        base = (c if kind == 0 else 1 - c) * HALF
        return remote(
            right_ref.at[0, j, pl.ds(pl.multiple_of(base, TILE), TILE),
                         pl.ds(pl.multiple_of(base + TILE, TILE), TILE)],
            corner.at[2 * j + kind], rsend.at[j, kind], drecv.at[2 * j + kind], target(kind))

    off_parts = ((0, 0, HALF), (TILE, 0, TILE), (TILE, TILE, TILE))

    def off_piece(slot, piece):
        r0, c0, width = off_parts[piece]
        return roff.at[slot, pl.ds(r0, TILE), pl.ds(c0, width)]

    def off_copy(j, piece):
        r0, c0, width = off_parts[piece]
        src = right_ref.at[0, j, pl.ds(r0, TILE), pl.ds(HALF + c0, width)]
        i = 2 * (piece - 1) + j
        if piece == 0 or i >= LONG_WAY:
            return remote(src, off_piece(2 * j, piece), rsend.at[j, 2 + (piece > 0)],
                          brecv.at[2 * j, piece], (before, t))
        return remote(src, passing.at[0, i], hsend.at[0, i], hrecv.at[0, i], (right, t))

    passed = []

    def pass_on(hop, i):
        src = passing.at[hop, i]
        remote(src, src, hsend.at[hop, i], hrecv.at[hop, i], other).wait_recv()
        if hop == 0:
            cp = remote(src, passing.at[1, i], hsend.at[1, i], hrecv.at[1, i], (right, t))
        else:
            j, piece = i % 2, 1 + i // 2
            cp = remote(src, off_piece(2 * j, piece), hsend.at[2, i], brecv.at[2 * j, piece],
                        (last_to, t))
        cp.start()
        passed.append(cp)

    def off_forward(j, piece):
        return remote(off_piece(2 * j, piece), off_piece(2 * j + 1, piece),
                      bfwd.at[j, piece], brecv.at[2 * j + 1, piece], other)

    def packed_copy(kind, u):
        return remote(packed_out.at[kind, u], packed.at[kind, u],
                      psend.at[kind, u], precv.at[kind, u], target(kind))

    def unpack(kind, u):
        both = packed[kind, u, pl.ds(0, TILE)]
        line = packed[kind, u, pl.ds(TILE, 8)][0:1]
        mirrored = both.T
        first = jnp.where(tile_row <= tile_col, both, mirrored)
        second = jnp.where(tile_row > tile_col, both, mirrored)
        return first, jnp.where(tile_row == tile_col, line, second)

    shifts = [off_copy(0, 1), off_copy(1, 1), off_copy(0, 2)]
    shifts += [off_copy(0, 0), corner_copy(0, 0), corner_copy(0, 1)]
    shifts += [packed_copy(0, 0), packed_copy(1, 0)]
    shifts += [off_copy(1, 0), corner_copy(1, 0), corner_copy(1, 1)]
    shifts += [packed_copy(0, 1), packed_copy(1, 1), off_copy(1, 2)]
    for cp in shifts:
        cp.start()
    left_cross = [
        remote(left_ref.at[0, j], lstage.at[2 * j + 1], lsend.at[j], lrecv.at[j], other)
        for j in range(2)
    ]
    for cp in left_cross:
        cp.start()

    row_index = lax.broadcasted_iota(jnp.int32, (ROWS, HALF), 0) + z * ROWS
    col_index = lax.broadcasted_iota(jnp.int32, (ROWS, HALF), 1) + c * HALF
    live = jnp.where(
        (row_index < dims_ref[0, 0]) & (col_index < dims_ref[0, 1]), 1.0, 0.0).astype(F32)

    own_rows = rows_of(z)

    def gather_start(n, u):
        def ring_copy(k, src_chip, index):
            piece = turned.at[n, 0, u, rows_of(src_chip)]
            return remote(piece, piece, ag_send.at[n, u], ag_recv.at[n, u, index], on_ring(k))

        def cross(k):
            rows = rows_of(chip(k))
            group = 0 if abs(k) <= 2 else 1
            remote(turned.at[n, 0, u, rows], turned.at[n, 1, u, rows],
                   cross_send.at[n, u], cross_recv.at[n, u, group], other).start()

        def received(index, k):
            piece = turned.at[n, 0, u, rows_of(chip(k))]
            remote(piece, piece, ag_send.at[n, u], ag_recv.at[n, u, index],
                   on_ring(k)).wait_recv()

        ring_copy(2, z, 0).start()
        ring_copy(-2, z, 1).start()
        ring_copy(1, z, 2).start()
        ring_copy(-1, z, 3).start()
        cross(0)

        def forward():
            received(0, -2)
            ring_copy(2, chip(-2), 5).start()
            ring_copy(1, chip(-2), 4).start()
            received(1, 2)
            ring_copy(-1, chip(2), 6).start()
            cross(-2)
            cross(2)
            received(2, -1)
            cross(-1)
            received(3, 1)
            cross(1)

        def finish():
            received(4, -3)
            cross(-3)
            received(6, 3)
            cross(3)
            received(5, -4)
            cross(-4)

        def complete(group):
            some = turned.at[n, 1, u, pl.ds(0, len(GROUPS[group]) * ROWS)]
            remote(some, some, cross_send.at[n, u], cross_recv.at[n, u, group],
                   other).wait_recv()

        return forward, finish, complete

    def gather_sent(n, u):
        seven = rsbuf.at[0, 0]
        remote(seven, seven, ag_send.at[n, u], ag_recv.at[n, u, 0], other).wait_send()
        half = turned.at[n, 0, u]
        remote(half, half, cross_send.at[n, u], cross_recv.at[n, u, 0], other).wait_send()

    def block(u, j):
        return part.at[u, pl.ds((j + 6) % RING * ROWS, ROWS)]

    def reduce_send(n, u, src, slot, k):
        remote(src, rsbuf.at[n, u, slot], rs_send.at[n, u], rs_recv.at[n, u, slot],
               on_ring(k)).start()

    def reduce_wait(n, u, slot):
        piece = rsbuf.at[n, u, slot]
        remote(piece, piece, rs_send.at[n, u], rs_recv.at[n, u, slot], on_ring(1)).wait_recv()

    def reduce_far(n, u):
        reduce_send(n, u, block(u, 4), 1, 2)
        reduce_send(n, u, block(u, 3), 0, 1)
        reduce_send(n, u, block(u, 5), 2, -1)

    def reduce_near(n, u):
        reduce_send(n, u, block(u, 1), 3, 1)
        reduce_send(n, u, block(u, 7), 4, -1)

    def reduce_relay(n, u):
        reduce_wait(n, u, 0)
        reduce_wait(n, u, 1)
        block(u, 2)[...] = block(u, 2)[...] + rsbuf[n, u, 0] + rsbuf[n, u, 1]
        reduce_send(n, u, block(u, 2), 5, 2)
        reduce_wait(n, u, 2)
        block(u, 6)[...] = block(u, 6)[...] + rsbuf[n, u, 2]
        reduce_send(n, u, block(u, 6), 6, -2)

    def reduce_final(n, u):
        reduce_wait(n, u, 3)
        reduce_wait(n, u, 4)
        total = block(u, 0)[...] + rsbuf[n, u, 3] + rsbuf[n, u, 4]
        reduce_wait(n, u, 5)
        reduce_wait(n, u, 6)
        return total + rsbuf[n, u, 5] + rsbuf[n, u, 6]

    def reduce_sent(n, u):
        seven = rsbuf.at[n, u]
        remote(seven, seven, rs_send.at[n, u], rs_recv.at[n, u, 0], other).wait_send()

    def own_image(n, u, vector):
        cols = slice(u * TILE, (u + 1) * TILE)
        turned[n + 1, 0, u, own_rows] = live[:, cols] * (
            reduce_final(n, u) + site[:, cols] * vector)

    def carry(q, u):
        cols = slice(u * TILE, (u + 1) * TILE)
        acc = None
        for k in range(2):
            new = (dot(vhi[k], rhi[q, k, :, cols]) + dot(vlo[k], rhi[q, k, :, cols])
                   + dot(vhi[k], rlo[q, k, :, cols]))
            acc = new if acc is None else acc + new
        chi[q, :, cols], clo[q, :, cols] = split(acc)

    def carry_rows(group):
        where = [rows_of(chip(k)) for k in GROUPS[group]]
        high = [jnp.concatenate([vhi[k, rows] for rows in where], axis=0) for k in range(2)]
        low = [jnp.concatenate([vlo[k, rows] for rows in where], axis=0) for k in range(2)]
        for q in range(4):
            acc = (dot(high[0], rhi[q, 0]) + dot(high[1], rhi[q, 1])
                   + dot(low[0], rhi[q, 0]) + dot(low[1], rhi[q, 1])
                   + dot(high[0], rlo[q, 0]) + dot(high[1], rlo[q, 1]))
            hi, lo = split(acc)
            for i, rows in enumerate(where):
                chi[q, rows] = hi[i * ROWS:(i + 1) * ROWS]
                clo[q, rows] = lo[i * ROWS:(i + 1) * ROWS]

    def bring_back(rows, cols):
        terms = [
            dot(lhi[q, rows], chi[q, :, cols]) + dot(llo[q, rows], chi[q, :, cols])
            + dot(lhi[q, rows], clo[q, :, cols])
            for q in range(4)
        ]
        return (terms[0] + terms[1]) + (terms[2] + terms[3])

    far_rows, near_rows = slice(0, HALF), slice(HALF, PAD)
    every = slice(0, HALF)

    def products(u):
        cols = slice(u * TILE, (u + 1) * TILE)
        part[u, far_rows] = bring_back(far_rows, cols)
        reduce_far(0, u)
        part[u, near_rows] = bring_back(near_rows, cols)
        reduce_near(0, u)

    def operate(after_far):
        for rows, then in ((far_rows, after_far), (near_rows, None)):
            fresh = bring_back(rows, every)
            for u in range(2):
                part[u, rows] = fresh[:, u * TILE:(u + 1) * TILE]
            if then is not None:
                then()

    CHUNK = 128

    def over_chunks(body, u):
        totals = []
        for half in range(2):
            def step(i, acc, half=half):
                value = body(half, u, pl.ds(pl.multiple_of(i * CHUNK, CHUNK), CHUNK))
                return acc + jnp.sum(value.reshape(CHUNK // 8, 8, TILE), axis=0)
            acc = lax.fori_loop(0, PAD // CHUNK, step, jnp.zeros((8, TILE), F32))
            totals.append(jnp.sum(acc, axis=(0, 1), keepdims=True))
        return totals

    def combine(first, second):
        return (first[0] + second[0]) + (first[1] + second[1])

    def store_split(half, u, rows, value):
        hi, lo = split(value)
        vhi[u, rows, pl.ds(half * TILE, TILE)] = hi
        vlo[u, rows, pl.ds(half * TILE, TILE)] = lo

    def bend_part(u, inverse):
        own = resid[0, u, own_rows] * inverse
        acc = site[:, u * TILE:(u + 1) * TILE] * own * own
        for k in range(RING):
            acc = acc + (block(u, k)[...] * inverse) * (
                resid[0, u, rows_of(chip(k))] * inverse)
        return jnp.sum(acc, axis=(0, 1), keepdims=True)

    def send_bend(n, mine):
        scal[n, t] = jnp.broadcast_to(mine, (1, TILE))
        for k in range(1, 2 * RING):
            remote(scal.at[n, t], scal.at[n, t], sc_send.at[n], sc_recv.at[n],
                   (s, lax.rem(t + k, 2 * RING))).start()

    def bend_total(n):
        others = scal.at[n, pl.ds(0, 2 * RING - 1)]
        remote(others, others, sc_send.at[n], sc_recv.at[n], other).wait()
        return jnp.sum(scal[n], axis=0)[:, 0:1]

    def coefficients(ritz, res_square, bend):
        half_gap = 0.5 * (bend - ritz)
        radius = jnp.sqrt(half_gap * half_gap + res_square)
        step = -jnp.sqrt(res_square) / (half_gap + radius)
        back = 1.0 / jnp.sqrt(1.0 + step * step)
        return step, back, ritz + half_gap - radius

    def absorb(n, group, scaled, back, ritz):
        for k in GROUPS[group]:
            rows = rows_of(chip(k))
            sums = []
            for half in range(2):
                total = []
                for u in range(2):
                    est = (estimate[half, u, rows] + scaled * resid[half, u, rows]) * back
                    img = (image[half, u, rows] + scaled * turned[n + 1, half, u, rows]) * back
                    estimate[half, u, rows] = est
                    image[half, u, rows] = img
                    res = img - ritz * est
                    resid[half, u, rows] = res
                    store_split(half, u, rows, res)
                    total.append(jnp.sum((res * res).reshape(ROWS // 8, 8, TILE), axis=0))
                sums.append(total[0] + total[1])
            squares[chip(k)] = sums[0] + sums[1]
        carry_rows(group)

    def take_in(n, phases, scaled, back, ritz):
        for forward, _, _ in phases:
            forward()
        for _, _, complete in phases:
            complete(0)
        absorb(n, 0, scaled, back, ritz)
        for _, finish, _ in phases:
            finish()
        for _, _, complete in phases:
            complete(1)
        absorb(n, 1, scaled, back, ritz)
        return jnp.sum(jnp.sum(squares[...], axis=0), axis=(0, 1), keepdims=True)

    for cp in inputs:
        cp.wait_send()
    inputs_in = [
        remote(buf.at[peer_rows], buf.at[peer_rows], insend.at[k], inrecv.at[k], other)
        for k, buf in enumerate((start, site))
    ]
    for cp in inputs_in:
        cp.wait_recv()
    start[my_rows] = init_ref[:, own_cols]
    site[my_rows] = site_ref[:, own_cols]
    masked = live * start[...]
    phases = []
    for u in range(2):
        turned[0, 0, u, own_rows] = masked[:, u * TILE:(u + 1) * TILE]
        phases.append(gather_start(0, u))
    pass_on(0, 0)
    pass_on(0, 1)
    for forward, _, _ in phases:
        forward()
    for hop, i in ((0, 2), (1, 0)):
        pass_on(hop, i)
    left_cross[0].wait()
    split_left(1)
    pass_on(1, 1)
    for _, finish, _ in phases:
        finish()
    left_cross[1].wait()
    split_left(3)
    pass_on(1, 2)

    def first_split(half, u, rows):
        value = turned[0, half, u, rows]
        zero = jnp.zeros_like(value)
        resid[half, u, rows] = value
        estimate[half, u, rows] = zero
        image[half, u, rows] = zero
        store_split(half, u, rows, value)
        return value * value

    present = jnp.where(s + 1 < SECTIONS, 1.0, 0.0).astype(F32)

    def arrived(ref, sem):
        remote(ref, ref, rsend.at[0, 0], sem, other).wait_recv()

    def put(q, k, half, u, value):
        hi, lo = split(value * present)
        rows, cols = pl.ds(half * TILE, TILE), pl.ds(u * TILE, TILE)
        rhi[q, k, rows, cols] = hi
        rlo[q, k, rows, cols] = lo

    def put_off(q, u):
        for k in range(2):
            @pl.when(c == 0)
            def _():
                put(q, k, 1, u, roff[q, pl.ds(u * TILE, TILE), pl.ds(k * TILE, TILE)].T)

            @pl.when(c == 1)
            def _():
                put(q, k, 1, u, roff[q, pl.ds(k * TILE, TILE), pl.ds(u * TILE, TILE)])

    def put_diag(u):
        for kind in range(2):
            arrived(packed.at[kind, u], precv.at[kind, u])
            for j, value in enumerate(unpack(kind, u)):
                put(2 * j + kind, u, 0, u, value)

    forwards = []

    def off_arrived(j, u):
        for piece in ((0, 1) if u == 0 else (2,)):
            arrived(off_piece(2 * j, piece), brecv.at[2 * j, piece])
            forwards.append(off_forward(j, piece))
            forwards[-1].start()

    def ready(j, u):
        off_arrived(j, u)
        for q in (2 * j, 2 * j + 1):
            if q % 2:
                for piece in ((0, 1) if u == 0 else (2,)):
                    arrived(off_piece(q, piece), brecv.at[q, piece])
            put_off(q, u)
            if u == 0:
                arrived(corner.at[q], drecv.at[q])
                put(q, 0, 0, 1, corner[q])
                put(q, 1, 0, 0, corner[q].T)

    ready(0, 0)
    put_diag(0)
    for _, _, complete in phases:
        complete(0)
        complete(1)
    norm_square = combine(over_chunks(first_split, 0), over_chunks(first_split, 1))
    inverse = 1.0 / jnp.sqrt(norm_square)
    carry(0, 0)
    carry(1, 0)
    ready(1, 0)
    carry(2, 0)
    carry(3, 0)
    products(0)
    bend_share = bend_part(0, inverse)
    put_diag(1)
    for j in range(2):
        ready(j, 1)
        carry(2 * j, 1)
        carry(2 * j + 1, 1)
    reduce_relay(0, 0)
    products(1)
    send_bend(0, bend_share + bend_part(1, inverse))
    own_image(0, 0, resid[0, 0, own_rows])
    phases = [gather_start(1, 0)]
    reduce_relay(0, 1)
    own_image(0, 1, resid[0, 1, own_rows])
    phases.append(gather_start(1, 1))
    ritz = bend_total(0)
    res_square = take_in(0, phases, inverse, 1.0, ritz)
    for cp in shifts + passed + forwards:
        cp.wait_send()
    for u in range(2):
        reduce_sent(0, u)

    def iterate(n, carried):
        ritz, res_square = carried
        inverse = 1.0 / jnp.sqrt(res_square)

        def send_far():
            for u in range(2):
                reduce_far(n, u)

        operate(send_far)
        for u in range(2):
            reduce_near(n, u)
        send_bend(n, bend_part(0, inverse) + bend_part(1, inverse))
        for u in range(2):
            reduce_relay(n, u)
        phases = []
        for u in range(2):
            own_image(n, u, resid[0, u, own_rows])
            phases.append(gather_start(n + 1, u))
        step, back, new_ritz = coefficients(ritz, res_square, bend_total(n))
        new_square = take_in(n, phases, step * inverse, back, new_ritz)
        for u in range(2):
            reduce_sent(n, u)
        return new_ritz, new_square

    ritz, res_square = lax.fori_loop(1, ITERS, iterate, (ritz, res_square))

    operate(None)
    inverse = 1.0 / jnp.sqrt(res_square)
    send_bend(ITERS, bend_part(0, inverse) + bend_part(1, inverse))
    step, back, ritz = coefficients(ritz, res_square, bend_total(ITERS))
    scaled = step * inverse
    out_rows = pl.ds(pl.multiple_of(t * (ROWS // 2), ROWS // 2), ROWS // 2)
    for half, base in ((0, c * HALF), (1, (1 - c) * HALF)):
        for u in range(2):
            est = (estimate[half, u, out_rows] + scaled * resid[half, u, out_rows]) * back
            cols = pl.ds(pl.multiple_of(base + u * TILE, TILE), TILE)
            out_ref[:, cols] = est * (0.5 * PAD)
    energy_ref[0] = ritz[0, 0]
    for n in range(ITERS + 1):
        for u in range(2):
            gather_sent(n, u)


def per_device(initial, onsite, left_env, right_env, sector_dims):
    vmem = pl.BlockSpec(memory_space=pltpu.VMEM)
    smem = pl.BlockSpec(memory_space=pltpu.SMEM)
    anywhere = pl.BlockSpec(memory_space=pl.ANY)
    dma = pltpu.SemaphoreType.DMA
    full = (2, 2, PAD, TILE)
    return pl.pallas_call(
        kernel,
        out_shape=(
            jax.ShapeDtypeStruct((ROWS // 2, PAD), F32),
            jax.ShapeDtypeStruct((1,), F32),
        ),
        in_specs=[vmem, vmem, anywhere, anywhere, smem],
        out_specs=(vmem, smem),
        scratch_shapes=[
            pltpu.VMEM((4, PAD, PAD), F32),
            pltpu.VMEM((4, PAD, PAD), BF16),
            pltpu.VMEM((4, PAD, PAD), BF16),
            pltpu.VMEM((2, 2, 2, TILE, TILE), F32),
            pltpu.VMEM((2, 2, TILE + 8, TILE), F32),
            pltpu.VMEM((2, 2, TILE + 8, TILE), F32),
            pltpu.VMEM((4, TILE, TILE), F32),
            pltpu.VMEM((4, HALF, HALF), F32),
            pltpu.VMEM((4, 2, HALF, HALF), BF16),
            pltpu.VMEM((4, 2, HALF, HALF), BF16),
            pltpu.VMEM((4, PAD, HALF), BF16),
            pltpu.VMEM((4, PAD, HALF), BF16),
            pltpu.VMEM((RING, 8, TILE), F32),
            pltpu.VMEM((2, LONG_WAY, TILE, TILE), F32),
            pltpu.VMEM((ROWS, HALF), F32),
            pltpu.VMEM((ROWS, HALF), F32),
            pltpu.VMEM((ITERS + 1,) + full, F32),
            pltpu.VMEM(full, F32),
            pltpu.VMEM(full, F32),
            pltpu.VMEM(full, F32),
            pltpu.VMEM((2, PAD, HALF), BF16),
            pltpu.VMEM((2, PAD, HALF), BF16),
            pltpu.VMEM((2, PAD, TILE), F32),
            pltpu.VMEM((ITERS, 2, 7, ROWS, TILE), F32),
            pltpu.VMEM((ITERS + 1, 2 * RING, 1, TILE), F32),
            dma((2,)), dma((2, 2, 2)), dma((2,)), dma((2,)), dma((2,)), dma((2,)),
            dma((2, 4)), dma((2, 2)), dma((2, 2)), dma((4,)), dma((4, 3)), dma((2, 3)),
            dma((3, LONG_WAY)), dma((2, LONG_WAY)),
            dma((ITERS, 2)), dma((ITERS, 2, 7)),
            dma((ITERS + 1, 2)), dma((ITERS + 1, 2, 7)),
            dma((ITERS + 1, 2)), dma((ITERS + 1, 2, 2)),
            dma((ITERS + 1,)), dma((ITERS + 1,)),
        ],
        compiler_params=pltpu.CompilerParams(
            collective_id=0, has_side_effects=True, vmem_limit_bytes=56 * 2**20),
        cost_estimate=pl.CostEstimate(
            flops=5 * 3 * 2 * 4 * 2 * PAD * PAD * HALF, bytes_accessed=2**23, transcendentals=0),
    )(initial, onsite, left_env, right_env, sector_dims)


def solution(mesh):
    return jax.shard_map(
        per_device,
        mesh=mesh,
        in_specs=(
            P(("sec", "term"), None),
            P(("sec", "term"), None),
            P("sec", "term", None, None),
            P("sec", "term", None, None),
            P("sec", None),
        ),
        out_specs=(P(("sec", "term"), None), P("sec")),
        check_vma=False,
    )
```

```python
import functools

import jax
import jax.numpy as jnp
from jax import lax
from jax.experimental import pallas as pl
from jax.experimental.pallas import tpu as pltpu
from jax.sharding import PartitionSpec as P

ITERS = 4
PAD = 512
HALF = 256
TILE = 128
RING = 8
SECTIONS = 16
GROUPS = ((0, -1, 1, -2, 2), (-3, 3, 4))
LONG_WAY = 3
SIDE = 4
ROWS = PAD // RING
MESH = pl.DeviceIdType.MESH
F32, BF16 = jnp.float32, jnp.bfloat16


def dot(a, b):
    return jnp.dot(a, b, preferred_element_type=F32)


def split(x):
    high = x.astype(BF16)
    return high, (x - high.astype(F32)).astype(BF16)


def kernel(
    init_ref, site_ref, left_ref, right_ref, dims_ref, out_ref, energy_ref,
    lstage, lhi, llo, tiles, packed_out, packed, corner, roff, rhi, rlo, chi, clo, squares, passing,
    start, site, turned, estimate, image, resid, vhi, vlo, part, rsbuf, scal,
    lsem, tsem, lsend, lrecv, insend, inrecv, rsend, psend, precv, drecv, brecv, bfwd, hsend, hrecv,
    rs_send, rs_recv, ag_send, ag_recv, cross_send, cross_recv, sc_send, sc_recv,
):
    s, t = lax.axis_index("sec"), lax.axis_index("term")
    z, c = t // 2, t % 2
    sign = 2 * c - 1

    def chip(k):
        return lax.rem(z + sign * k + 2 * RING, RING)

    def on_ring(k):
        return (s, chip(k) * 2 + c)

    other = (s, z * 2 + 1 - c)
    before = lax.rem(s + SECTIONS - 1, SECTIONS)
    after = lax.rem(s + 1, SECTIONS)
    x, y = s % SIDE, s // SIDE

    def section_at(x_of, y_of):
        return lax.rem(y_of + SIDE, SIDE) * SIDE + lax.rem(x_of + SIDE, SIDE)

    right, left = section_at(x + 1, y), section_at(x - 1, y)
    last_to = section_at(x + 1, y - (x == SIDE - 2).astype(jnp.int32))
    last_from = section_at(x - 1, y + (x == SIDE - 1).astype(jnp.int32))

    def rows_of(chip_index):
        return pl.ds(pl.multiple_of(chip_index * ROWS, ROWS), ROWS)

    def remote(src, dst, send, recv, to):
        return pltpu.make_async_remote_copy(
            src_ref=src, dst_ref=dst, send_sem=send, recv_sem=recv,
            device_id=to, device_id_type=MESH,
        )

    local_left = [
        pltpu.make_async_copy(left_ref.at[0, j], lstage.at[2 * j], lsem.at[j])
        for j in range(2)
    ]
    for cp in local_left:
        cp.start()

    def tile_copy(j, kind, u):
        base = pl.multiple_of((c if kind == 0 else 1 - c) * HALF + u * TILE, TILE)
        return pltpu.make_async_copy(
            right_ref.at[0, j, pl.ds(base, TILE), pl.ds(base, TILE)],
            tiles.at[j, kind, u], tsem.at[j, kind, u])

    for u in range(2):
        for kind in range(2):
            for j in range(2):
                tile_copy(j, kind, u).start()

    barrier = pltpu.get_barrier_semaphore()
    greeted = [on_ring(k) for k in (1, -1, 2, -2)] + [other]
    greeted += [(after, z * 2 + k) for k in range(2)] + [(left, t), (last_from, t)]
    for device in greeted:
        pl.semaphore_signal(barrier, inc=1, device_id=device, device_id_type=MESH)
    tile_row = lax.broadcasted_iota(jnp.int32, (TILE, TILE), 0)
    tile_col = lax.broadcasted_iota(jnp.int32, (TILE, TILE), 1)

    def pack(kind, u):
        for j in range(2):
            tile_copy(j, kind, u).wait()
        second = tiles[1, kind, u]
        packed_out[kind, u, pl.ds(0, TILE)] = jnp.where(
            tile_row <= tile_col, tiles[0, kind, u], second)
        line = jnp.sum(jnp.where(tile_row == tile_col, second, 0.0), axis=0, keepdims=True)
        packed_out[kind, u, pl.ds(TILE, 8)] = jnp.broadcast_to(line, (8, TILE))

    def split_left(q):
        for k in range(RING):
            hi, lo = split(lstage[q, rows_of(chip(k + 2))])
            lhi[q, pl.ds(k * ROWS, ROWS)] = hi
            llo[q, pl.ds(k * ROWS, ROWS)] = lo

    for u in range(2):
        for kind in range(2):
            pack(kind, u)
    for j in range(2):
        local_left[j].wait()
        split_left(2 * j)
    pl.semaphore_wait(barrier, len(greeted))

    own_cols = pl.ds(pl.multiple_of(c * HALF, HALF), HALF)
    other_cols = pl.ds(pl.multiple_of((1 - c) * HALF, HALF), HALF)
    my_rows = pl.ds(pl.multiple_of(c * (ROWS // 2), ROWS // 2), ROWS // 2)
    peer_rows = pl.ds(pl.multiple_of((1 - c) * (ROWS // 2), ROWS // 2), ROWS // 2)
    inputs = [
        remote(ref.at[:, other_cols], buf.at[my_rows], insend.at[k], inrecv.at[k], other)
        for k, (ref, buf) in enumerate(((init_ref, start), (site_ref, site)))
    ]
    for cp in inputs:
        cp.start()

    def target(kind):
        return (before, z * 2 + (c if kind == 0 else 1 - c))

    def corner_copy(j, kind):
        base = (c if kind == 0 else 1 - c) * HALF
        return remote(
            right_ref.at[0, j, pl.ds(pl.multiple_of(base, TILE), TILE),
                         pl.ds(pl.multiple_of(base + TILE, TILE), TILE)],
            corner.at[2 * j + kind], rsend.at[j, kind], drecv.at[2 * j + kind], target(kind))

    off_parts = ((0, 0, HALF), (TILE, 0, TILE), (TILE, TILE, TILE))

    def off_piece(slot, piece):
        r0, c0, width = off_parts[piece]
        return roff.at[slot, pl.ds(r0, TILE), pl.ds(c0, width)]

    def off_copy(j, piece):
        r0, c0, width = off_parts[piece]
        src = right_ref.at[0, j, pl.ds(r0, TILE), pl.ds(HALF + c0, width)]
        i = 2 * (piece - 1) + j
        if piece == 0 or i >= LONG_WAY:
            return remote(src, off_piece(2 * j, piece), rsend.at[j, 2 + (piece > 0)],
                          brecv.at[2 * j, piece], (before, t))
        return remote(src, passing.at[0, i], hsend.at[0, i], hrecv.at[0, i], (right, t))

    passed = []

    def pass_on(hop, i):
        src = passing.at[hop, i]
        remote(src, src, hsend.at[hop, i], hrecv.at[hop, i], other).wait_recv()
        if hop == 0:
            cp = remote(src, passing.at[1, i], hsend.at[1, i], hrecv.at[1, i], (right, t))
        else:
            j, piece = i % 2, 1 + i // 2
            cp = remote(src, off_piece(2 * j, piece), hsend.at[2, i], brecv.at[2 * j, piece],
                        (last_to, t))
        cp.start()
        passed.append(cp)

    def off_forward(j, piece):
        return remote(off_piece(2 * j, piece), off_piece(2 * j + 1, piece),
                      bfwd.at[j, piece], brecv.at[2 * j + 1, piece], other)

    def packed_copy(kind, u):
        return remote(packed_out.at[kind, u], packed.at[kind, u],
                      psend.at[kind, u], precv.at[kind, u], target(kind))

    def unpack(kind, u):
        both = packed[kind, u, pl.ds(0, TILE)]
        line = packed[kind, u, pl.ds(TILE, 8)][0:1]
        mirrored = both.T
        first = jnp.where(tile_row <= tile_col, both, mirrored)
        second = jnp.where(tile_row > tile_col, both, mirrored)
        return first, jnp.where(tile_row == tile_col, line, second)

    shifts = [off_copy(0, 1), off_copy(1, 1), off_copy(0, 2)]
    shifts += [off_copy(0, 0), corner_copy(0, 0), corner_copy(0, 1)]
    shifts += [packed_copy(0, 0), packed_copy(1, 0)]
    shifts += [off_copy(1, 0), corner_copy(1, 0), corner_copy(1, 1)]
    shifts += [off_copy(1, 2), packed_copy(0, 1), packed_copy(1, 1)]
    for cp in shifts:
        cp.start()
    left_cross = [
        remote(left_ref.at[0, j], lstage.at[2 * j + 1], lsend.at[j], lrecv.at[j], other)
        for j in range(2)
    ]
    for cp in left_cross:
        cp.start()

    row_index = lax.broadcasted_iota(jnp.int32, (ROWS, HALF), 0) + z * ROWS
    col_index = lax.broadcasted_iota(jnp.int32, (ROWS, HALF), 1) + c * HALF
    live = jnp.where(
        (row_index < dims_ref[0, 0]) & (col_index < dims_ref[0, 1]), 1.0, 0.0).astype(F32)

    own_rows = rows_of(z)

    def gather_start(n, u):
        def ring_copy(k, src_chip, index):
            piece = turned.at[n, 0, u, rows_of(src_chip)]
            return remote(piece, piece, ag_send.at[n, u], ag_recv.at[n, u, index], on_ring(k))

        def cross(k):
            rows = rows_of(chip(k))
            group = 0 if abs(k) <= 2 else 1
            remote(turned.at[n, 0, u, rows], turned.at[n, 1, u, rows],
                   cross_send.at[n, u], cross_recv.at[n, u, group], other).start()

        def received(index, k):
            piece = turned.at[n, 0, u, rows_of(chip(k))]
            remote(piece, piece, ag_send.at[n, u], ag_recv.at[n, u, index],
                   on_ring(k)).wait_recv()

        ring_copy(2, z, 0).start()
        ring_copy(-2, z, 1).start()
        ring_copy(1, z, 2).start()
        ring_copy(-1, z, 3).start()
        cross(0)

        def forward():
            received(0, -2)
            ring_copy(2, chip(-2), 5).start()
            ring_copy(1, chip(-2), 4).start()
            received(1, 2)
            ring_copy(-1, chip(2), 6).start()
            cross(-2)
            cross(2)
            received(2, -1)
            cross(-1)
            received(3, 1)
            cross(1)

        def finish():
            received(4, -3)
            cross(-3)
            received(6, 3)
            cross(3)
            received(5, -4)
            cross(-4)

        def complete(group):
            some = turned.at[n, 1, u, pl.ds(0, len(GROUPS[group]) * ROWS)]
            remote(some, some, cross_send.at[n, u], cross_recv.at[n, u, group],
                   other).wait_recv()

        return forward, finish, complete

    def gather_sent(n, u):
        seven = rsbuf.at[0, 0]
        remote(seven, seven, ag_send.at[n, u], ag_recv.at[n, u, 0], other).wait_send()
        half = turned.at[n, 0, u]
        remote(half, half, cross_send.at[n, u], cross_recv.at[n, u, 0], other).wait_send()

    def block(u, j):
        return part.at[u, pl.ds((j + 6) % RING * ROWS, ROWS)]

    def reduce_send(n, u, src, slot, k):
        remote(src, rsbuf.at[n, u, slot], rs_send.at[n, u], rs_recv.at[n, u, slot],
               on_ring(k)).start()

    def reduce_wait(n, u, slot):
        piece = rsbuf.at[n, u, slot]
        remote(piece, piece, rs_send.at[n, u], rs_recv.at[n, u, slot], on_ring(1)).wait_recv()

    def reduce_far(n, u):
        reduce_send(n, u, block(u, 4), 1, 2)
        reduce_send(n, u, block(u, 3), 0, 1)
        reduce_send(n, u, block(u, 5), 2, -1)

    def reduce_near(n, u):
        reduce_send(n, u, block(u, 1), 3, 1)
        reduce_send(n, u, block(u, 7), 4, -1)

    def reduce_relay(n, u):
        reduce_wait(n, u, 2)
        block(u, 6)[...] = block(u, 6)[...] + rsbuf[n, u, 2]
        reduce_send(n, u, block(u, 6), 6, -2)
        reduce_wait(n, u, 0)
        reduce_wait(n, u, 1)
        block(u, 2)[...] = block(u, 2)[...] + rsbuf[n, u, 0] + rsbuf[n, u, 1]
        reduce_send(n, u, block(u, 2), 5, 2)

    def reduce_final(n, u):
        reduce_wait(n, u, 3)
        reduce_wait(n, u, 4)
        total = block(u, 0)[...] + rsbuf[n, u, 3] + rsbuf[n, u, 4]
        reduce_wait(n, u, 5)
        reduce_wait(n, u, 6)
        return total + rsbuf[n, u, 5] + rsbuf[n, u, 6]

    def reduce_sent(n, u):
        seven = rsbuf.at[n, u]
        remote(seven, seven, rs_send.at[n, u], rs_recv.at[n, u, 0], other).wait_send()

    def own_image(n, u, vector):
        cols = slice(u * TILE, (u + 1) * TILE)
        turned[n + 1, 0, u, own_rows] = live[:, cols] * (
            reduce_final(n, u) + site[:, cols] * vector)

    def carry(q, u):
        cols = slice(u * TILE, (u + 1) * TILE)
        acc = None
        for k in range(2):
            new = (dot(vhi[k], rhi[q, k, :, cols]) + dot(vlo[k], rhi[q, k, :, cols])
                   + dot(vhi[k], rlo[q, k, :, cols]))
            acc = new if acc is None else acc + new
        chi[q, :, cols], clo[q, :, cols] = split(acc)

    def carry_rows(group):
        where = [rows_of(chip(k)) for k in GROUPS[group]]
        high = [jnp.concatenate([vhi[k, rows] for rows in where], axis=0) for k in range(2)]
        low = [jnp.concatenate([vlo[k, rows] for rows in where], axis=0) for k in range(2)]
        for q in range(4):
            acc = (dot(high[0], rhi[q, 0]) + dot(high[1], rhi[q, 1])
                   + dot(low[0], rhi[q, 0]) + dot(low[1], rhi[q, 1])
                   + dot(high[0], rlo[q, 0]) + dot(high[1], rlo[q, 1]))
            hi, lo = split(acc)
            for i, rows in enumerate(where):
                chi[q, rows] = hi[i * ROWS:(i + 1) * ROWS]
                clo[q, rows] = lo[i * ROWS:(i + 1) * ROWS]

    def bring_back(rows, cols):
        terms = [
            dot(lhi[q, rows], chi[q, :, cols]) + dot(llo[q, rows], chi[q, :, cols])
            + dot(lhi[q, rows], clo[q, :, cols])
            for q in range(4)
        ]
        return (terms[0] + terms[1]) + (terms[2] + terms[3])

    far_rows, near_rows = slice(0, HALF), slice(HALF, PAD)
    every = slice(0, HALF)

    def products(u):
        cols = slice(u * TILE, (u + 1) * TILE)
        part[u, far_rows] = bring_back(far_rows, cols)
        reduce_far(0, u)
        part[u, near_rows] = bring_back(near_rows, cols)
        reduce_near(0, u)

    def operate(after_far):
        for rows, then in ((far_rows, after_far), (near_rows, lambda: None)):
            fresh = bring_back(rows, every)
            for u in range(2):
                part[u, rows] = fresh[:, u * TILE:(u + 1) * TILE]
            then()

    CHUNK = 128

    def over_chunks(body, u):
        totals = []
        for half in range(2):
            def step(i, acc, half=half):
                value = body(half, u, pl.ds(pl.multiple_of(i * CHUNK, CHUNK), CHUNK))
                return acc + jnp.sum(value.reshape(CHUNK // 8, 8, TILE), axis=0)
            acc = lax.fori_loop(0, PAD // CHUNK, step, jnp.zeros((8, TILE), F32))
            totals.append(jnp.sum(acc, axis=(0, 1), keepdims=True))
        return totals

    def combine(first, second):
        return (first[0] + second[0]) + (first[1] + second[1])

    def store_split(half, u, rows, value):
        hi, lo = split(value)
        vhi[u, rows, pl.ds(half * TILE, TILE)] = hi
        vlo[u, rows, pl.ds(half * TILE, TILE)] = lo

    def bend_part(u, inverse):
        own = resid[0, u, own_rows] * inverse
        acc = site[:, u * TILE:(u + 1) * TILE] * own * own
        for k in range(RING):
            acc = acc + (block(u, k)[...] * inverse) * (
                resid[0, u, rows_of(chip(k))] * inverse)
        return jnp.sum(acc, axis=(0, 1), keepdims=True)

    def send_bend(n, mine):
        scal[n, t] = jnp.broadcast_to(mine, (1, TILE))
        for k in range(1, 2 * RING):
            remote(scal.at[n, t], scal.at[n, t], sc_send.at[n], sc_recv.at[n],
                   (s, lax.rem(t + k, 2 * RING))).start()

    def bend_total(n):
        others = scal.at[n, pl.ds(0, 2 * RING - 1)]
        remote(others, others, sc_send.at[n], sc_recv.at[n], other).wait()
        return jnp.sum(scal[n], axis=0)[:, 0:1]

    def coefficients(ritz, res_square, bend):
        half_gap = 0.5 * (bend - ritz)
        radius = jnp.sqrt(half_gap * half_gap + res_square)
        step = -jnp.sqrt(res_square) / (half_gap + radius)
        back = 1.0 / jnp.sqrt(1.0 + step * step)
        return step, back, ritz + half_gap - radius

    def absorb(n, group, scaled, back, ritz):
        for k in GROUPS[group]:
            rows = rows_of(chip(k))
            sums = []
            for half in range(2):
                total = []
                for u in range(2):
                    est = (estimate[half, u, rows] + scaled * resid[half, u, rows]) * back
                    img = (image[half, u, rows] + scaled * turned[n + 1, half, u, rows]) * back
                    estimate[half, u, rows] = est
                    image[half, u, rows] = img
                    res = img - ritz * est
                    resid[half, u, rows] = res
                    store_split(half, u, rows, res)
                    total.append(jnp.sum((res * res).reshape(ROWS // 8, 8, TILE), axis=0))
                sums.append(total[0] + total[1])
            squares[chip(k)] = sums[0] + sums[1]
        carry_rows(group)

    def take_in(n, phases, scaled, back, ritz):
        for forward, _, _ in phases:
            forward()
        for _, _, complete in phases:
            complete(0)
        absorb(n, 0, scaled, back, ritz)
        for _, finish, _ in phases:
            finish()
        for _, _, complete in phases:
            complete(1)
        absorb(n, 1, scaled, back, ritz)
        return jnp.sum(jnp.sum(squares[...], axis=0), axis=(0, 1), keepdims=True)

    for cp in inputs:
        cp.wait_send()
    inputs_in = [
        remote(buf.at[peer_rows], buf.at[peer_rows], insend.at[k], inrecv.at[k], other)
        for k, buf in enumerate((start, site))
    ]
    for cp in inputs_in:
        cp.wait_recv()
    start[my_rows] = init_ref[:, own_cols]
    site[my_rows] = site_ref[:, own_cols]
    masked = live * start[...]
    phases = []
    for u in range(2):
        turned[0, 0, u, own_rows] = masked[:, u * TILE:(u + 1) * TILE]
        phases.append(gather_start(0, u))
    pass_on(0, 0)
    pass_on(0, 1)
    for forward, _, _ in phases:
        forward()
    for hop, i in ((0, 2), (1, 0)):
        pass_on(hop, i)
    left_cross[0].wait()
    split_left(1)
    pass_on(1, 1)
    for _, finish, _ in phases:
        finish()
    left_cross[1].wait()
    split_left(3)
    pass_on(1, 2)

    def first_split(half, u, rows):
        value = turned[0, half, u, rows]
        zero = jnp.zeros_like(value)
        resid[half, u, rows] = value
        estimate[half, u, rows] = zero
        image[half, u, rows] = zero
        store_split(half, u, rows, value)
        return value * value

    present = jnp.where(s + 1 < SECTIONS, 1.0, 0.0).astype(F32)

    def arrived(ref, sem):
        remote(ref, ref, rsend.at[0, 0], sem, other).wait_recv()

    def put(q, k, half, u, value):
        hi, lo = split(value * present)
        rows, cols = pl.ds(half * TILE, TILE), pl.ds(u * TILE, TILE)
        rhi[q, k, rows, cols] = hi
        rlo[q, k, rows, cols] = lo

    def put_off(q, u):
        for k in range(2):
            @pl.when(c == 0)
            def _():
                put(q, k, 1, u, roff[q, pl.ds(u * TILE, TILE), pl.ds(k * TILE, TILE)].T)

            @pl.when(c == 1)
            def _():
                put(q, k, 1, u, roff[q, pl.ds(k * TILE, TILE), pl.ds(u * TILE, TILE)])

    def put_diag(u):
        for kind in range(2):
            arrived(packed.at[kind, u], precv.at[kind, u])
            for j, value in enumerate(unpack(kind, u)):
                put(2 * j + kind, u, 0, u, value)

    forwards = []

    def off_arrived(j, u):
        for piece in ((0, 1) if u == 0 else (2,)):
            arrived(off_piece(2 * j, piece), brecv.at[2 * j, piece])
            forwards.append(off_forward(j, piece))
            forwards[-1].start()

    def ready(j, u):
        off_arrived(j, u)
        for q in (2 * j, 2 * j + 1):
            if q % 2:
                for piece in ((0, 1) if u == 0 else (2,)):
                    arrived(off_piece(q, piece), brecv.at[q, piece])
            put_off(q, u)
            if u == 0:
                arrived(corner.at[q], drecv.at[q])
                put(q, 0, 0, 1, corner[q])
                put(q, 1, 0, 0, corner[q].T)

    ready(0, 0)
    put_diag(0)
    for _, _, complete in phases:
        complete(0)
        complete(1)
    norm_square = combine(over_chunks(first_split, 0), over_chunks(first_split, 1))
    inverse = 1.0 / jnp.sqrt(norm_square)
    carry(0, 0)
    carry(1, 0)
    ready(1, 0)
    carry(2, 0)
    carry(3, 0)
    products(0)
    bend_share = bend_part(0, inverse)
    for j in range(2):
        ready(j, 1)
    put_diag(1)
    for q in range(4):
        carry(q, 1)
    reduce_relay(0, 0)
    products(1)
    send_bend(0, bend_share + bend_part(1, inverse))
    own_image(0, 0, resid[0, 0, own_rows])
    phases = [gather_start(1, 0)]
    reduce_relay(0, 1)
    own_image(0, 1, resid[0, 1, own_rows])
    phases.append(gather_start(1, 1))
    ritz = bend_total(0)
    res_square = take_in(0, phases, inverse, 1.0, ritz)
    for cp in shifts + passed + forwards:
        cp.wait_send()
    for u in range(2):
        reduce_sent(0, u)

    def iterate(n, carried):
        ritz, res_square = carried
        inverse = 1.0 / jnp.sqrt(res_square)

        def send_far():
            for u in range(2):
                reduce_far(n, u)

        operate(send_far)
        for u in range(2):
            reduce_near(n, u)
        send_bend(n, bend_part(0, inverse) + bend_part(1, inverse))
        for u in range(2):
            reduce_relay(n, u)
        phases = []
        for u in range(2):
            own_image(n, u, resid[0, u, own_rows])
            phases.append(gather_start(n + 1, u))
        step, back, new_ritz = coefficients(ritz, res_square, bend_total(n))
        new_square = take_in(n, phases, step * inverse, back, new_ritz)
        for u in range(2):
            reduce_sent(n, u)
        return new_ritz, new_square

    ritz, res_square = lax.fori_loop(1, ITERS, iterate, (ritz, res_square))

    operate(lambda: None)
    inverse = 1.0 / jnp.sqrt(res_square)
    send_bend(ITERS, bend_part(0, inverse) + bend_part(1, inverse))
    step, back, ritz = coefficients(ritz, res_square, bend_total(ITERS))
    scaled = step * inverse
    out_rows = pl.ds(pl.multiple_of(t * (ROWS // 2), ROWS // 2), ROWS // 2)
    for half, base in ((0, c * HALF), (1, (1 - c) * HALF)):
        for u in range(2):
            est = (estimate[half, u, out_rows] + scaled * resid[half, u, out_rows]) * back
            cols = pl.ds(pl.multiple_of(base + u * TILE, TILE), TILE)
            out_ref[:, cols] = est * (0.5 * PAD)
    energy_ref[0] = ritz[0, 0]
    for n in range(ITERS + 1):
        for u in range(2):
            gather_sent(n, u)


def per_device(initial, onsite, left_env, right_env, sector_dims):
    vmem = pl.BlockSpec(memory_space=pltpu.VMEM)
    smem = pl.BlockSpec(memory_space=pltpu.SMEM)
    anywhere = pl.BlockSpec(memory_space=pl.ANY)
    dma = pltpu.SemaphoreType.DMA
    full = (2, 2, PAD, TILE)
    return pl.pallas_call(
        kernel,
        out_shape=(
            jax.ShapeDtypeStruct((ROWS // 2, PAD), F32),
            jax.ShapeDtypeStruct((1,), F32),
        ),
        in_specs=[vmem, vmem, anywhere, anywhere, smem],
        out_specs=(vmem, smem),
        scratch_shapes=[
            pltpu.VMEM((4, PAD, PAD), F32),
            pltpu.VMEM((4, PAD, PAD), BF16),
            pltpu.VMEM((4, PAD, PAD), BF16),
            pltpu.VMEM((2, 2, 2, TILE, TILE), F32),
            pltpu.VMEM((2, 2, TILE + 8, TILE), F32),
            pltpu.VMEM((2, 2, TILE + 8, TILE), F32),
            pltpu.VMEM((4, TILE, TILE), F32),
            pltpu.VMEM((4, HALF, HALF), F32),
            pltpu.VMEM((4, 2, HALF, HALF), BF16),
            pltpu.VMEM((4, 2, HALF, HALF), BF16),
            pltpu.VMEM((4, PAD, HALF), BF16),
            pltpu.VMEM((4, PAD, HALF), BF16),
            pltpu.VMEM((RING, 8, TILE), F32),
            pltpu.VMEM((2, LONG_WAY, TILE, TILE), F32),
            pltpu.VMEM((ROWS, HALF), F32),
            pltpu.VMEM((ROWS, HALF), F32),
            pltpu.VMEM((ITERS + 1,) + full, F32),
            pltpu.VMEM(full, F32),
            pltpu.VMEM(full, F32),
            pltpu.VMEM(full, F32),
            pltpu.VMEM((2, PAD, HALF), BF16),
            pltpu.VMEM((2, PAD, HALF), BF16),
            pltpu.VMEM((2, PAD, TILE), F32),
            pltpu.VMEM((ITERS, 2, 7, ROWS, TILE), F32),
            pltpu.VMEM((ITERS + 1, 2 * RING, 1, TILE), F32),
            dma((2,)), dma((2, 2, 2)), dma((2,)), dma((2,)), dma((2,)), dma((2,)),
            dma((2, 4)), dma((2, 2)), dma((2, 2)), dma((4,)), dma((4, 3)), dma((2, 3)),
            dma((3, LONG_WAY)), dma((2, LONG_WAY)),
            dma((ITERS, 2)), dma((ITERS, 2, 7)),
            dma((ITERS + 1, 2)), dma((ITERS + 1, 2, 7)),
            dma((ITERS + 1, 2)), dma((ITERS + 1, 2, 2)),
            dma((ITERS + 1,)), dma((ITERS + 1,)),
        ],
        compiler_params=pltpu.CompilerParams(
            collective_id=0, has_side_effects=True, vmem_limit_bytes=56 * 2**20),
        cost_estimate=pl.CostEstimate(
            flops=5 * 3 * 2 * 4 * 2 * PAD * PAD * HALF, bytes_accessed=2**23, transcendentals=0),
    )(initial, onsite, left_env, right_env, sector_dims)


def solution(mesh):
    return jax.shard_map(
        per_device,
        mesh=mesh,
        in_specs=(
            P(("sec", "term"), None),
            P(("sec", "term"), None),
            P("sec", "term", None, None),
            P("sec", "term", None, None),
            P("sec", None),
        ),
        out_specs=(P(("sec", "term"), None), P("sec")),
        check_vma=False,
    )
```

```python
import functools

import jax
import jax.numpy as jnp
from jax import lax
from jax.experimental import pallas as pl
from jax.experimental.pallas import tpu as pltpu
from jax.sharding import PartitionSpec as P

ITERS = 4
PAD = 512
HALF = 256
TILE = 128
RING = 8
SECTIONS = 16
GROUPS = ((0, -1, 1, -2, 2), (-3, 3, 4))
LONG_WAY = 3
SIDE = 4
ROWS = PAD // RING
MESH = pl.DeviceIdType.MESH
F32, BF16 = jnp.float32, jnp.bfloat16


def dot(a, b):
    return jnp.dot(a, b, preferred_element_type=F32)


def split(x):
    high = x.astype(BF16)
    return high, (x - high.astype(F32)).astype(BF16)


def kernel(
    init_ref, site_ref, left_ref, right_ref, dims_ref, out_ref, energy_ref,
    lstage, lhi, llo, tiles, packed_out, packed, corner, roff, rhi, rlo, chi, clo, squares, passing,
    start, site, turned, estimate, image, resid, vhi, vlo, part, rsbuf, scal,
    lsem, tsem, lsend, lrecv, insend, inrecv, rsend, psend, precv, drecv, brecv, bfwd, hsend, hrecv,
    rs_send, rs_recv, ag_send, ag_recv, cross_send, cross_recv, sc_send, sc_recv,
):
    s, t = lax.axis_index("sec"), lax.axis_index("term")
    z, c = t // 2, t % 2
    sign = 2 * c - 1

    def chip(k):
        return lax.rem(z + sign * k + 2 * RING, RING)

    def on_ring(k):
        return (s, chip(k) * 2 + c)

    other = (s, z * 2 + 1 - c)
    before = lax.rem(s + SECTIONS - 1, SECTIONS)
    after = lax.rem(s + 1, SECTIONS)
    x, y = s % SIDE, s // SIDE

    def section_at(x_of, y_of):
        return lax.rem(y_of + SIDE, SIDE) * SIDE + lax.rem(x_of + SIDE, SIDE)

    right, left = section_at(x + 1, y), section_at(x - 1, y)
    last_to = section_at(x + 1, y - (x == SIDE - 2).astype(jnp.int32))
    last_from = section_at(x - 1, y + (x == SIDE - 1).astype(jnp.int32))

    def rows_of(chip_index):
        return pl.ds(pl.multiple_of(chip_index * ROWS, ROWS), ROWS)

    def remote(src, dst, send, recv, to):
        return pltpu.make_async_remote_copy(
            src_ref=src, dst_ref=dst, send_sem=send, recv_sem=recv,
            device_id=to, device_id_type=MESH,
        )

    local_left = [
        pltpu.make_async_copy(left_ref.at[0, j], lstage.at[2 * j], lsem.at[j])
        for j in range(2)
    ]
    for cp in local_left:
        cp.start()

    def tile_copy(j, kind, u):
        base = pl.multiple_of((c if kind == 0 else 1 - c) * HALF + u * TILE, TILE)
        return pltpu.make_async_copy(
            right_ref.at[0, j, pl.ds(base, TILE), pl.ds(base, TILE)],
            tiles.at[j, kind, u], tsem.at[j, kind, u])

    for u in range(2):
        for kind in range(2):
            for j in range(2):
                tile_copy(j, kind, u).start()

    barrier = pltpu.get_barrier_semaphore()
    greeted = [on_ring(k) for k in (1, -1, 2, -2)] + [other]
    greeted += [(after, z * 2 + k) for k in range(2)] + [(left, t), (last_from, t)]
    for device in greeted:
        pl.semaphore_signal(barrier, inc=1, device_id=device, device_id_type=MESH)
    tile_row = lax.broadcasted_iota(jnp.int32, (TILE, TILE), 0)
    tile_col = lax.broadcasted_iota(jnp.int32, (TILE, TILE), 1)

    def pack(kind, u):
        for j in range(2):
            tile_copy(j, kind, u).wait()
        second = tiles[1, kind, u]
        packed_out[kind, u, pl.ds(0, TILE)] = jnp.where(
            tile_row <= tile_col, tiles[0, kind, u], second)
        line = jnp.sum(jnp.where(tile_row == tile_col, second, 0.0), axis=0, keepdims=True)
        packed_out[kind, u, pl.ds(TILE, 8)] = jnp.broadcast_to(line, (8, TILE))

    def split_left(q):
        for k in range(RING):
            hi, lo = split(lstage[q, rows_of(chip(k + 2))])
            lhi[q, pl.ds(k * ROWS, ROWS)] = hi
            llo[q, pl.ds(k * ROWS, ROWS)] = lo

    for u in range(2):
        for kind in range(2):
            pack(kind, u)
    for j in range(2):
        local_left[j].wait()
        split_left(2 * j)
    pl.semaphore_wait(barrier, len(greeted))

    own_cols = pl.ds(pl.multiple_of(c * HALF, HALF), HALF)
    other_cols = pl.ds(pl.multiple_of((1 - c) * HALF, HALF), HALF)
    my_rows = pl.ds(pl.multiple_of(c * (ROWS // 2), ROWS // 2), ROWS // 2)
    peer_rows = pl.ds(pl.multiple_of((1 - c) * (ROWS // 2), ROWS // 2), ROWS // 2)
    inputs = [
        remote(ref.at[:, other_cols], buf.at[my_rows], insend.at[k], inrecv.at[k], other)
        for k, (ref, buf) in enumerate(((init_ref, start), (site_ref, site)))
    ]
    for cp in inputs:
        cp.start()

    def target(kind):
        return (before, z * 2 + (c if kind == 0 else 1 - c))

    def corner_copy(j, kind):
        base = (c if kind == 0 else 1 - c) * HALF
        return remote(
            right_ref.at[0, j, pl.ds(pl.multiple_of(base, TILE), TILE),
                         pl.ds(pl.multiple_of(base + TILE, TILE), TILE)],
            corner.at[2 * j + kind], rsend.at[j, kind], drecv.at[2 * j + kind], target(kind))

    off_parts = ((0, 0, HALF), (TILE, 0, TILE), (TILE, TILE, TILE))

    def off_piece(slot, piece):
        r0, c0, width = off_parts[piece]
        return roff.at[slot, pl.ds(r0, TILE), pl.ds(c0, width)]

    def off_copy(j, piece):
        r0, c0, width = off_parts[piece]
        src = right_ref.at[0, j, pl.ds(r0, TILE), pl.ds(HALF + c0, width)]
        i = 2 * (piece - 1) + j
        if piece == 0 or i >= LONG_WAY:
            return remote(src, off_piece(2 * j, piece), rsend.at[j, 2 + (piece > 0)],
                          brecv.at[2 * j, piece], (before, t))
        return remote(src, passing.at[0, i], hsend.at[0, i], hrecv.at[0, i], (right, t))

    passed = []

    def pass_on(hop, i):
        src = passing.at[hop, i]
        remote(src, src, hsend.at[hop, i], hrecv.at[hop, i], other).wait_recv()
        if hop == 0:
            cp = remote(src, passing.at[1, i], hsend.at[1, i], hrecv.at[1, i], (right, t))
        else:
            j, piece = i % 2, 1 + i // 2
            cp = remote(src, off_piece(2 * j, piece), hsend.at[2, i], brecv.at[2 * j, piece],
                        (last_to, t))
        cp.start()
        passed.append(cp)

    def off_forward(j, piece):
        return remote(off_piece(2 * j, piece), off_piece(2 * j + 1, piece),
                      bfwd.at[j, piece], brecv.at[2 * j + 1, piece], other)

    def packed_copy(kind, u):
        return remote(packed_out.at[kind, u], packed.at[kind, u],
                      psend.at[kind, u], precv.at[kind, u], target(kind))

    def unpack(kind, u):
        both = packed[kind, u, pl.ds(0, TILE)]
        line = packed[kind, u, pl.ds(TILE, 8)][0:1]
        mirrored = both.T
        first = jnp.where(tile_row <= tile_col, both, mirrored)
        second = jnp.where(tile_row > tile_col, both, mirrored)
        return first, jnp.where(tile_row == tile_col, line, second)

    shifts = [off_copy(0, 1), off_copy(1, 1), off_copy(0, 2)]
    shifts += [off_copy(0, 0), corner_copy(0, 0), corner_copy(0, 1)]
    shifts += [packed_copy(0, 0), packed_copy(1, 0)]
    shifts += [off_copy(1, 0), corner_copy(1, 0), corner_copy(1, 1)]
    shifts += [off_copy(1, 2), packed_copy(0, 1), packed_copy(1, 1)]
    for cp in shifts:
        cp.start()
    left_cross = [
        remote(left_ref.at[0, j], lstage.at[2 * j + 1], lsend.at[j], lrecv.at[j], other)
        for j in range(2)
    ]
    for cp in left_cross:
        cp.start()

    row_index = lax.broadcasted_iota(jnp.int32, (ROWS, HALF), 0) + z * ROWS
    col_index = lax.broadcasted_iota(jnp.int32, (ROWS, HALF), 1) + c * HALF
    live = jnp.where(
        (row_index < dims_ref[0, 0]) & (col_index < dims_ref[0, 1]), 1.0, 0.0).astype(F32)

    own_rows = rows_of(z)

    def gather_start(n, u):
        def ring_copy(k, src_chip, index):
            piece = turned.at[n, 0, u, rows_of(src_chip)]
            return remote(piece, piece, ag_send.at[n, u], ag_recv.at[n, u, index], on_ring(k))

        def cross(k):
            rows = rows_of(chip(k))
            group = 0 if abs(k) <= 2 else 1
            remote(turned.at[n, 0, u, rows], turned.at[n, 1, u, rows],
                   cross_send.at[n, u], cross_recv.at[n, u, group], other).start()

        def received(index, k):
            piece = turned.at[n, 0, u, rows_of(chip(k))]
            remote(piece, piece, ag_send.at[n, u], ag_recv.at[n, u, index],
                   on_ring(k)).wait_recv()

        ring_copy(2, z, 0).start()
        ring_copy(-2, z, 1).start()
        ring_copy(1, z, 2).start()
        ring_copy(-1, z, 3).start()
        cross(0)

        def forward():
            received(0, -2)
            ring_copy(2, chip(-2), 5).start()
            ring_copy(1, chip(-2), 4).start()
            received(1, 2)
            ring_copy(-1, chip(2), 6).start()
            cross(-2)
            cross(2)
            received(2, -1)
            cross(-1)
            received(3, 1)
            cross(1)

        def finish():
            received(4, -3)
            cross(-3)
            received(6, 3)
            cross(3)
            received(5, -4)
            cross(-4)

        def complete(group):
            some = turned.at[n, 1, u, pl.ds(0, len(GROUPS[group]) * ROWS)]
            remote(some, some, cross_send.at[n, u], cross_recv.at[n, u, group],
                   other).wait_recv()

        return forward, finish, complete

    def gather_sent(n, u):
        seven = rsbuf.at[0, 0]
        remote(seven, seven, ag_send.at[n, u], ag_recv.at[n, u, 0], other).wait_send()
        half = turned.at[n, 0, u]
        remote(half, half, cross_send.at[n, u], cross_recv.at[n, u, 0], other).wait_send()

    def block(u, j):
        return part.at[u, pl.ds((j + 6) % RING * ROWS, ROWS)]

    def reduce_send(n, u, src, slot, k):
        remote(src, rsbuf.at[n, u, slot], rs_send.at[n, u], rs_recv.at[n, u, slot],
               on_ring(k)).start()

    def reduce_wait(n, u, slot):
        piece = rsbuf.at[n, u, slot]
        remote(piece, piece, rs_send.at[n, u], rs_recv.at[n, u, slot], on_ring(1)).wait_recv()

    def reduce_far(n, u):
        reduce_send(n, u, block(u, 4), 1, 2)
        reduce_send(n, u, block(u, 3), 0, 1)
        reduce_send(n, u, block(u, 5), 2, -1)

    def reduce_near(n, u):
        reduce_send(n, u, block(u, 1), 3, 1)
        reduce_send(n, u, block(u, 7), 4, -1)

    def reduce_relay(n, u):
        reduce_wait(n, u, 2)
        block(u, 6)[...] = block(u, 6)[...] + rsbuf[n, u, 2]
        reduce_send(n, u, block(u, 6), 6, -2)
        reduce_wait(n, u, 0)
        reduce_wait(n, u, 1)
        block(u, 2)[...] = block(u, 2)[...] + rsbuf[n, u, 0] + rsbuf[n, u, 1]
        reduce_send(n, u, block(u, 2), 5, 2)

    def reduce_final(n, u):
        reduce_wait(n, u, 3)
        reduce_wait(n, u, 4)
        total = block(u, 0)[...] + rsbuf[n, u, 3] + rsbuf[n, u, 4]
        reduce_wait(n, u, 5)
        reduce_wait(n, u, 6)
        return total + rsbuf[n, u, 5] + rsbuf[n, u, 6]

    def reduce_sent(n, u):
        seven = rsbuf.at[n, u]
        remote(seven, seven, rs_send.at[n, u], rs_recv.at[n, u, 0], other).wait_send()

    def own_image(n, u, vector):
        cols = slice(u * TILE, (u + 1) * TILE)
        turned[n + 1, 0, u, own_rows] = live[:, cols] * (
            reduce_final(n, u) + site[:, cols] * vector)

    def carry(q, u):
        cols = slice(u * TILE, (u + 1) * TILE)
        acc = None
        for k in range(2):
            new = (dot(vhi[k], rhi[q, k, :, cols]) + dot(vlo[k], rhi[q, k, :, cols])
                   + dot(vhi[k], rlo[q, k, :, cols]))
            acc = new if acc is None else acc + new
        chi[q, :, cols], clo[q, :, cols] = split(acc)

    def carry_rows(group):
        where = [rows_of(chip(k)) for k in GROUPS[group]]
        high = [jnp.concatenate([vhi[k, rows] for rows in where], axis=0) for k in range(2)]
        low = [jnp.concatenate([vlo[k, rows] for rows in where], axis=0) for k in range(2)]
        for q in range(4):
            acc = (dot(high[0], rhi[q, 0]) + dot(high[1], rhi[q, 1])
                   + dot(low[0], rhi[q, 0]) + dot(low[1], rhi[q, 1])
                   + dot(high[0], rlo[q, 0]) + dot(high[1], rlo[q, 1]))
            hi, lo = split(acc)
            for i, rows in enumerate(where):
                chi[q, rows] = hi[i * ROWS:(i + 1) * ROWS]
                clo[q, rows] = lo[i * ROWS:(i + 1) * ROWS]

    def bring_back(rows, cols):
        terms = [
            dot(lhi[q, rows], chi[q, :, cols]) + dot(llo[q, rows], chi[q, :, cols])
            + dot(lhi[q, rows], clo[q, :, cols])
            for q in range(4)
        ]
        return (terms[0] + terms[1]) + (terms[2] + terms[3])

    far_rows, near_rows = slice(0, HALF), slice(HALF, PAD)
    every = slice(0, HALF)

    def operate(after_far):
        for rows, then in ((far_rows, after_far), (near_rows, lambda: None)):
            fresh = bring_back(rows, every)
            for u in range(2):
                part[u, rows] = fresh[:, u * TILE:(u + 1) * TILE]
            then()

    CHUNK = 128

    def over_chunks(body, u):
        totals = []
        for half in range(2):
            def step(i, acc, half=half):
                value = body(half, u, pl.ds(pl.multiple_of(i * CHUNK, CHUNK), CHUNK))
                return acc + jnp.sum(value.reshape(CHUNK // 8, 8, TILE), axis=0)
            acc = lax.fori_loop(0, PAD // CHUNK, step, jnp.zeros((8, TILE), F32))
            totals.append(jnp.sum(acc, axis=(0, 1), keepdims=True))
        return totals

    def combine(first, second):
        return (first[0] + second[0]) + (first[1] + second[1])

    def store_split(half, u, rows, value):
        hi, lo = split(value)
        vhi[u, rows, pl.ds(half * TILE, TILE)] = hi
        vlo[u, rows, pl.ds(half * TILE, TILE)] = lo

    def bend_part(u, inverse):
        own = resid[0, u, own_rows] * inverse
        acc = site[:, u * TILE:(u + 1) * TILE] * own * own
        for k in range(RING):
            acc = acc + (block(u, k)[...] * inverse) * (
                resid[0, u, rows_of(chip(k))] * inverse)
        return jnp.sum(acc, axis=(0, 1), keepdims=True)

    def send_bend(n, mine):
        scal[n, t] = jnp.broadcast_to(mine, (1, TILE))
        for k in range(1, 2 * RING):
            remote(scal.at[n, t], scal.at[n, t], sc_send.at[n], sc_recv.at[n],
                   (s, lax.rem(t + k, 2 * RING))).start()

    def bend_total(n):
        others = scal.at[n, pl.ds(0, 2 * RING - 1)]
        remote(others, others, sc_send.at[n], sc_recv.at[n], other).wait()
        return jnp.sum(scal[n], axis=0)[:, 0:1]

    def coefficients(ritz, res_square, bend):
        half_gap = 0.5 * (bend - ritz)
        radius = jnp.sqrt(half_gap * half_gap + res_square)
        step = -jnp.sqrt(res_square) / (half_gap + radius)
        back = 1.0 / jnp.sqrt(1.0 + step * step)
        return step, back, ritz + half_gap - radius

    def absorb(n, group, scaled, back, ritz):
        for k in GROUPS[group]:
            rows = rows_of(chip(k))
            sums = []
            for half in range(2):
                total = []
                for u in range(2):
                    est = (estimate[half, u, rows] + scaled * resid[half, u, rows]) * back
                    img = (image[half, u, rows] + scaled * turned[n + 1, half, u, rows]) * back
                    estimate[half, u, rows] = est
                    image[half, u, rows] = img
                    res = img - ritz * est
                    resid[half, u, rows] = res
                    store_split(half, u, rows, res)
                    total.append(jnp.sum((res * res).reshape(ROWS // 8, 8, TILE), axis=0))
                sums.append(total[0] + total[1])
            squares[chip(k)] = sums[0] + sums[1]
        carry_rows(group)

    def take_in(n, phases, scaled, back, ritz):
        for forward, _, _ in phases:
            forward()
        for _, _, complete in phases:
            complete(0)
        absorb(n, 0, scaled, back, ritz)
        for _, finish, _ in phases:
            finish()
        for _, _, complete in phases:
            complete(1)
        absorb(n, 1, scaled, back, ritz)
        return jnp.sum(jnp.sum(squares[...], axis=0), axis=(0, 1), keepdims=True)

    for cp in inputs:
        cp.wait_send()
    inputs_in = [
        remote(buf.at[peer_rows], buf.at[peer_rows], insend.at[k], inrecv.at[k], other)
        for k, buf in enumerate((start, site))
    ]
    for cp in inputs_in:
        cp.wait_recv()
    start[my_rows] = init_ref[:, own_cols]
    site[my_rows] = site_ref[:, own_cols]
    masked = live * start[...]
    phases = []
    for u in range(2):
        turned[0, 0, u, own_rows] = masked[:, u * TILE:(u + 1) * TILE]
        phases.append(gather_start(0, u))
    pass_on(0, 0)
    pass_on(0, 1)
    for forward, _, _ in phases:
        forward()
    for hop, i in ((0, 2), (1, 0)):
        pass_on(hop, i)
    left_cross[0].wait()
    split_left(1)
    pass_on(1, 1)
    for _, finish, _ in phases:
        finish()
    left_cross[1].wait()
    split_left(3)
    pass_on(1, 2)

    def first_split(half, u, rows):
        value = turned[0, half, u, rows]
        zero = jnp.zeros_like(value)
        resid[half, u, rows] = value
        estimate[half, u, rows] = zero
        image[half, u, rows] = zero
        store_split(half, u, rows, value)
        return value * value

    present = jnp.where(s + 1 < SECTIONS, 1.0, 0.0).astype(F32)

    def arrived(ref, sem):
        remote(ref, ref, rsend.at[0, 0], sem, other).wait_recv()

    def put(q, k, half, u, value):
        hi, lo = split(value * present)
        rows, cols = pl.ds(half * TILE, TILE), pl.ds(u * TILE, TILE)
        rhi[q, k, rows, cols] = hi
        rlo[q, k, rows, cols] = lo

    def put_off(q, u):
        for k in range(2):
            @pl.when(c == 0)
            def _():
                put(q, k, 1, u, roff[q, pl.ds(u * TILE, TILE), pl.ds(k * TILE, TILE)].T)

            @pl.when(c == 1)
            def _():
                put(q, k, 1, u, roff[q, pl.ds(k * TILE, TILE), pl.ds(u * TILE, TILE)])

    def put_diag(u):
        for kind in range(2):
            arrived(packed.at[kind, u], precv.at[kind, u])
            for j, value in enumerate(unpack(kind, u)):
                put(2 * j + kind, u, 0, u, value)

    forwards = []

    def off_arrived(j, u):
        for piece in ((0, 1) if u == 0 else (2,)):
            arrived(off_piece(2 * j, piece), brecv.at[2 * j, piece])
            forwards.append(off_forward(j, piece))
            forwards[-1].start()

    def ready(j, u):
        off_arrived(j, u)
        for q in (2 * j, 2 * j + 1):
            if q % 2:
                for piece in ((0, 1) if u == 0 else (2,)):
                    arrived(off_piece(q, piece), brecv.at[q, piece])
            put_off(q, u)
            if u == 0:
                arrived(corner.at[q], drecv.at[q])
                put(q, 0, 0, 1, corner[q])
                put(q, 1, 0, 0, corner[q].T)

    ready(0, 0)
    put_diag(0)
    for _, _, complete in phases:
        complete(0)
        complete(1)
    norm_square = combine(over_chunks(first_split, 0), over_chunks(first_split, 1))
    inverse = 1.0 / jnp.sqrt(norm_square)
    carry(0, 0)
    carry(1, 0)
    ready(1, 0)
    carry(2, 0)
    carry(3, 0)
    for j in range(2):
        ready(j, 1)
    put_diag(1)
    for q in range(4):
        carry(q, 1)

    def send_first():
        for u in range(2):
            reduce_far(0, u)

    operate(send_first)
    for u in range(2):
        reduce_near(0, u)
    send_bend(0, bend_part(0, inverse) + bend_part(1, inverse))
    for u in range(2):
        reduce_relay(0, u)
    phases = []
    for u in range(2):
        own_image(0, u, resid[0, u, own_rows])
        phases.append(gather_start(1, u))
    ritz = bend_total(0)
    res_square = take_in(0, phases, inverse, 1.0, ritz)
    for cp in shifts + passed + forwards:
        cp.wait_send()
    for u in range(2):
        reduce_sent(0, u)

    def iterate(n, carried):
        ritz, res_square = carried
        inverse = 1.0 / jnp.sqrt(res_square)

        def send_far():
            for u in range(2):
                reduce_far(n, u)

        operate(send_far)
        for u in range(2):
            reduce_near(n, u)
        send_bend(n, bend_part(0, inverse) + bend_part(1, inverse))
        for u in range(2):
            reduce_relay(n, u)
        phases = []
        for u in range(2):
            own_image(n, u, resid[0, u, own_rows])
            phases.append(gather_start(n + 1, u))
        step, back, new_ritz = coefficients(ritz, res_square, bend_total(n))
        new_square = take_in(n, phases, step * inverse, back, new_ritz)
        for u in range(2):
            reduce_sent(n, u)
        return new_ritz, new_square

    ritz, res_square = lax.fori_loop(1, ITERS, iterate, (ritz, res_square))

    operate(lambda: None)
    inverse = 1.0 / jnp.sqrt(res_square)
    send_bend(ITERS, bend_part(0, inverse) + bend_part(1, inverse))
    step, back, ritz = coefficients(ritz, res_square, bend_total(ITERS))
    scaled = step * inverse
    out_rows = pl.ds(pl.multiple_of(t * (ROWS // 2), ROWS // 2), ROWS // 2)
    for half, base in ((0, c * HALF), (1, (1 - c) * HALF)):
        for u in range(2):
            est = (estimate[half, u, out_rows] + scaled * resid[half, u, out_rows]) * back
            cols = pl.ds(pl.multiple_of(base + u * TILE, TILE), TILE)
            out_ref[:, cols] = est * (0.5 * PAD)
    energy_ref[0] = ritz[0, 0]
    for n in range(ITERS + 1):
        for u in range(2):
            gather_sent(n, u)


def per_device(initial, onsite, left_env, right_env, sector_dims):
    vmem = pl.BlockSpec(memory_space=pltpu.VMEM)
    smem = pl.BlockSpec(memory_space=pltpu.SMEM)
    anywhere = pl.BlockSpec(memory_space=pl.ANY)
    dma = pltpu.SemaphoreType.DMA
    full = (2, 2, PAD, TILE)
    return pl.pallas_call(
        kernel,
        out_shape=(
            jax.ShapeDtypeStruct((ROWS // 2, PAD), F32),
            jax.ShapeDtypeStruct((1,), F32),
        ),
        in_specs=[vmem, vmem, anywhere, anywhere, smem],
        out_specs=(vmem, smem),
        scratch_shapes=[
            pltpu.VMEM((4, PAD, PAD), F32),
            pltpu.VMEM((4, PAD, PAD), BF16),
            pltpu.VMEM((4, PAD, PAD), BF16),
            pltpu.VMEM((2, 2, 2, TILE, TILE), F32),
            pltpu.VMEM((2, 2, TILE + 8, TILE), F32),
            pltpu.VMEM((2, 2, TILE + 8, TILE), F32),
            pltpu.VMEM((4, TILE, TILE), F32),
            pltpu.VMEM((4, HALF, HALF), F32),
            pltpu.VMEM((4, 2, HALF, HALF), BF16),
            pltpu.VMEM((4, 2, HALF, HALF), BF16),
            pltpu.VMEM((4, PAD, HALF), BF16),
            pltpu.VMEM((4, PAD, HALF), BF16),
            pltpu.VMEM((RING, 8, TILE), F32),
            pltpu.VMEM((2, LONG_WAY, TILE, TILE), F32),
            pltpu.VMEM((ROWS, HALF), F32),
            pltpu.VMEM((ROWS, HALF), F32),
            pltpu.VMEM((ITERS + 1,) + full, F32),
            pltpu.VMEM(full, F32),
            pltpu.VMEM(full, F32),
            pltpu.VMEM(full, F32),
            pltpu.VMEM((2, PAD, HALF), BF16),
            pltpu.VMEM((2, PAD, HALF), BF16),
            pltpu.VMEM((2, PAD, TILE), F32),
            pltpu.VMEM((ITERS, 2, 7, ROWS, TILE), F32),
            pltpu.VMEM((ITERS + 1, 2 * RING, 1, TILE), F32),
            dma((2,)), dma((2, 2, 2)), dma((2,)), dma((2,)), dma((2,)), dma((2,)),
            dma((2, 4)), dma((2, 2)), dma((2, 2)), dma((4,)), dma((4, 3)), dma((2, 3)),
            dma((3, LONG_WAY)), dma((2, LONG_WAY)),
            dma((ITERS, 2)), dma((ITERS, 2, 7)),
            dma((ITERS + 1, 2)), dma((ITERS + 1, 2, 7)),
            dma((ITERS + 1, 2)), dma((ITERS + 1, 2, 2)),
            dma((ITERS + 1,)), dma((ITERS + 1,)),
        ],
        compiler_params=pltpu.CompilerParams(
            collective_id=0, has_side_effects=True, vmem_limit_bytes=56 * 2**20),
        cost_estimate=pl.CostEstimate(
            flops=5 * 3 * 2 * 4 * 2 * PAD * PAD * HALF, bytes_accessed=2**23, transcendentals=0),
    )(initial, onsite, left_env, right_env, sector_dims)


def solution(mesh):
    return jax.shard_map(
        per_device,
        mesh=mesh,
        in_specs=(
            P(("sec", "term"), None),
            P(("sec", "term"), None),
            P("sec", "term", None, None),
            P("sec", "term", None, None),
            P("sec", None),
        ),
        out_specs=(P(("sec", "term"), None), P("sec")),
        check_vma=False,
    )
```
